512 devices in a mesh: dp: 16 (over y, z_lo), space: 32 (over x, z_hi, core).
Axes of the slice: x: 4, y: 4, z: 16 (z_hi: 4, z_lo: 4; z = z_hi * 4 + z_lo), core: 2. Of those that a mesh axis runs over, the one named last changes fastest.
Arguments:
- layer_input: bfloat16 [32, 32, 64, 4096], P('dp', None, None, 'space'), may hold values from -6 to 6
- cotangent: bfloat16 [32, 32, 64, 4096], P('dp', None, None, 'space'), may hold values from -6 to 6
- closure_step: int32 [32], P('dp'), may hold values from 0 to 31
- spectral_weight: float32 [64, 16, 2, 1024], P('space'), may hold values from -0.75 to 0.75
- point_weight: float32 [32, 32], replicated, may hold values from -1 to 1
- bias: float32 [32], replicated, may hold values from -4 to 4
Outputs:
- grad_input: bfloat16 [32, 32, 64, 4096], P('dp', None, None, 'space')
- grad_spectral: float32 [64, 16, 2, 1024], P('space')
- grad_point: float32 [32, 32], replicated
- grad_bias: float32 [32], replicated
The draws below stay inside these ranges and needn't reach their ends.
All inputs are finite; a program needn't handle non-finite values.
Results may differ from the reference program's by a relative error of at most 0.001.
Values sent between devices are 32-bit elements; how exact they have to be, the bound alone decides.
A program may use at most 128 MiB of HBM per device.

```python
import math
import jax
import jax.numpy as jnp
from jax import lax

C = 32
KX = 64
KT = 16
TSTEPS = 64
NX = 4096
SAMPLES = 32


def place_ends(drawn, own_key, low, largest):
    longest = drawn.shape.index(max(drawn.shape))
    spots = []
    for shift in (0, 1):
        where = [jax.random.randint(jax.random.fold_in(own_key, axis), (), 0, length) for axis, length in enumerate(drawn.shape)]
        where[longest] = (where[longest] + shift) % drawn.shape[longest]
        spots.append(tuple(where))
    return drawn.at[spots[0]].set(low).at[spots[1]].set(largest)


def block_levels(own_key, extent, cuts, least, high):
    def one(axis_at, blocks):
        heights = jax.random.uniform(jax.random.fold_in(jax.random.fold_in(own_key, 6), axis_at), (blocks,), jnp.float32, least / len(cuts), high / len(cuts))
        return jnp.repeat(jnp.exp(heights), extent[axis_at] // blocks).reshape((-1,) + (1,) * (len(extent) - axis_at - 1))

    factor_of = one(*cuts[0])
    for cut in cuts[1:]:
        factor_of = factor_of * one(*cut)
    return factor_of


def normal_values(stream_key, shape, width, reach, cuts=(), held_as=jnp.bfloat16):
    entries = jax.random.normal(stream_key, shape, jnp.float32) * width
    if len(cuts) > 0:
        entries = block_levels(stream_key, shape, cuts, -0.22, 0.18) * entries
    return jnp.clip(entries, min=-reach, max=reach).astype(held_as)


def setup_inputs(seed: int = 0) -> dict:
    key_of = jax.random.split(jax.random.key(seed), 7)
    return {
        "layer_input": normal_values(key_of[0], (SAMPLES, C, TSTEPS, NX), 1.0, 6.0, ((0, 16), (3, 32))),
        "cotangent": normal_values(key_of[1], (SAMPLES, C, TSTEPS, NX), 1.0, 6.0, ((0, 16), (3, 32))),
        "closure_step": place_ends(jax.random.randint(key_of[2], (SAMPLES,), 0, TSTEPS // 2), jax.random.fold_in(key_of[2], 1), 0, (TSTEPS // 2) - 1).astype(jnp.int32),
        "spectral_weight": normal_values(key_of[3], (KX, KT, 2, C * C), (2 * C) ** -0.5, 0.75, ((0, 32),), jnp.float32),
        "point_weight": normal_values(key_of[4], (C, C), C ** -0.5, 1.0, (), jnp.float32),
        "bias": normal_values(key_of[5], (C,), 1.0, 4.0, (), jnp.float32),
    }


PRECISE = lax.Precision.HIGHEST

def contract(form, left, right):
    return jnp.einsum(form, left, right, precision=PRECISE)

def space_frequency(number):
    indices = jnp.arange(number, dtype=jnp.int32)
    return jnp.where(indices >= number // 2, indices - number, indices)

def wave_table(frequency, positions, period):
    product = frequency[:, None] * positions[None, :] % period
    angles = product.astype(jnp.float32) * (2.0 * math.pi / period)
    return (jnp.cos(angles), jnp.sin(angles))

def forward_modes(values, tables):
    cos_x, sin_x, cos_t, sin_t = tables
    along_a = contract('ctx,mt->cmx', values, cos_t)
    along_b = contract('ctx,mt->cmx', values, sin_t)
    real_part = contract('cmx,jx->cjm', along_a, cos_x) - contract('cmx,jx->cjm', along_b, sin_x)
    imag_part = -(contract('cmx,jx->cjm', along_a, sin_x) + contract('cmx,jx->cjm', along_b, cos_x))
    return (real_part, imag_part)

def inverse_modes(real_part, imag_part, tables):
    cos_x, sin_x, cos_t, sin_t = tables
    upper = contract('cjm,jx->cmx', real_part, cos_x) - contract('cjm,jx->cmx', imag_part, sin_x)
    lower = contract('cjm,jx->cmx', real_part, sin_x) + contract('cjm,jx->cmx', imag_part, cos_x)
    return contract('cmx,mt->ctx', upper, cos_t) - contract('cmx,mt->ctx', lower, sin_t)

def reference(layer_input, cotangent, closure_step, spectral_weight, point_weight, bias):
    cos_x, sin_x = wave_table(space_frequency(KX), jnp.arange(NX, dtype=jnp.int32), NX)
    cos_t, sin_t = wave_table(jnp.arange(KT, dtype=jnp.int32), jnp.arange(TSTEPS, dtype=jnp.int32), TSTEPS)
    tables = (cos_x, sin_x, cos_t, sin_t)
    w_real = spectral_weight[:, :, 0].reshape(KX, KT, C, C)
    w_imag = spectral_weight[:, :, 1].reshape(KX, KT, C, C)
    in_scale = 1.0 / math.sqrt(NX * TSTEPS)
    out_scale = 1.0 / math.sqrt(KX * KT)
    time_index = jnp.arange(TSTEPS, dtype=jnp.int32)

    def per_sample(totals, inputs):
        sample_field, cot_slice, closure = inputs
        sample_field = sample_field.astype(jnp.float32)
        x_real, x_imag = forward_modes(sample_field, tables)
        x_real = x_real * in_scale
        x_imag = x_imag * in_scale
        y_real = contract('jmio,ijm->ojm', w_real, x_real) - contract('jmio,ijm->ojm', w_imag, x_imag)
        y_imag = contract('jmio,ijm->ojm', w_real, x_imag) + contract('jmio,ijm->ojm', w_imag, x_real)
        spectral = inverse_modes(y_real, y_imag, tables) * out_scale
        preact = spectral + contract('itx,io->otx', sample_field, point_weight) + bias[:, None, None]
        live_steps = (time_index >= closure).astype(jnp.float32)
        masked = cot_slice.astype(jnp.float32) * live_steps[None, :, None]
        unused, pullback = jax.vjp(jax.nn.gelu, preact)
        grad_pre = pullback(masked)[0]
        g_real, g_imag = forward_modes(grad_pre, tables)
        g_real = g_real * out_scale
        g_imag = g_imag * out_scale
        h_real = contract('jmio,ojm->ijm', w_real, g_real) + contract('jmio,ojm->ijm', w_imag, g_imag)
        h_imag = contract('jmio,ojm->ijm', w_real, g_imag) - contract('jmio,ojm->ijm', w_imag, g_real)
        grad_field = contract('otx,io->itx', grad_pre, point_weight) + inverse_modes(h_real, h_imag, tables) * in_scale
        dw_real = contract('ijm,ojm->jmio', x_real, g_real) + contract('ijm,ojm->jmio', x_imag, g_imag)
        dw_imag = contract('ijm,ojm->jmio', x_real, g_imag) - contract('ijm,ojm->jmio', x_imag, g_real)
        d_point = contract('itx,otx->io', sample_field, grad_pre)
        d_bias = lax.optimization_barrier(jnp.sum(grad_pre, axis=(1, 2)))
        new_totals = (totals[0] + dw_real, totals[1] + dw_imag, totals[2] + d_point, totals[3] + d_bias)
        return (new_totals, grad_field.astype(jnp.bfloat16))
    start_totals = (jnp.zeros((KX, KT, C, C), jnp.float32), jnp.zeros((KX, KT, C, C), jnp.float32), jnp.zeros((C, C), jnp.float32), jnp.zeros((C,), jnp.float32))
    totals, grad_input = lax.scan(per_sample, start_totals, (layer_input, cotangent, closure_step))
    sample_scale = 1.0 / math.sqrt(SAMPLES)
    point_scale = 1.0 / math.sqrt(SAMPLES * TSTEPS * NX)
    grad_spectral = jnp.stack([totals[0], totals[1]], 2).reshape(KX, KT, 2, C * C) * sample_scale
    return (grad_input, grad_spectral, totals[2] * point_scale, totals[3] * point_scale)
```

```python
import functools
import math

import jax
import jax.numpy as jnp
from jax import lax
from jax.experimental import pallas as pl
from jax.experimental.pallas import tpu as pltpu
from jax.sharding import PartitionSpec as P

F32 = jnp.float32
BF16 = jnp.bfloat16
S, C, T, X, M = 2, 32, 64, 128, 16
GROUPS = 32
NX = X * GROUPS
NN = (((1,), (0,)), ((), ()))
NT = (((1,), (1,)), ((), ()))
TWO_PI = 2.0 * math.pi
POINT_SCALE = 1.0 / math.sqrt(32 * T * NX)
SAMPLE_SCALE = 1.0 / math.sqrt(32)
IN_SCALE = 1.0 / 512.0
OUT_SCALE = 1.0 / 32.0
GELU_C = math.sqrt(2.0 / math.pi)


def iota(shape, axis):
    return lax.broadcasted_iota(jnp.int32, shape, axis)


def split(v):
    hi = v.astype(BF16)
    return hi, (v - hi.astype(F32)).astype(BF16)


def dot(a, b, dims=NN):
    return lax.dot_general(a, b, dims, preferred_element_type=F32)


def dot3(a, b, dims=NN):
    return dot(a[0], b[0], dims) + (dot(a[0], b[1], dims) + dot(a[1], b[0], dims))


def dot_exact(a, b, dims=NN):
    return lax.dot_general(a, b, dims, preferred_element_type=F32, precision=lax.Precision.HIGHEST)


def one_hot_product(rows, table):
    hi, lo = split(rows)
    n = rows.shape[0]
    both = dot(jnp.concatenate([hi, lo], axis=0), table)
    return both[:n] + both[n:]


def kernel(
    u_hbm, c_hbm, step_ref, w_hbm, pw_ref, bias_ref,
    out_hbm, dw_out, point_out, bias_out,
    u, cot, wv, pre, gp, ob,
    d1, d2, d3, d4, k1, k2, rep, rept, tile, tilet, bcol, onehot,
    ab, ul, xr, accp, accb,
    rs0, rc0, rs1, rx, rs2, rz, ag,
    dw, ry, dw1, rzl, dwf,
    small, sc_, sx, sz, sy, szl,
    local_sem, send_sem, recv_sem,
):
    dp = lax.axis_index("dp")
    sp = lax.axis_index("space")
    core = lax.rem(sp, 2)
    zh = lax.rem(sp // 2, 4)
    xx = sp // 8
    yy = dp // 4
    zl = lax.rem(dp, 4)

    def device(x=xx, z=zh, c=core, y=yy, l=zl):
        return (y * 4 + l, x * 8 + z * 2 + c)

    def peer(axis, d):
        if axis == "core":
            return device(c=1 - core)
        if axis == "x":
            return device(x=lax.rem(xx + d, 4))
        if axis == "z":
            return device(z=lax.rem(zh + d, 4))
        if axis == "y":
            return device(y=lax.rem(yy + d, 4))
        return device(l=lax.rem(zl + d, 4))

    def distances(axis):
        return (1,) if axis == "core" else (1, 2, 3)

    loads = [
        pltpu.make_async_copy(u_hbm.at[0], u.at[0], local_sem.at[0]),
        pltpu.make_async_copy(u_hbm.at[1], u.at[1], local_sem.at[1]),
        pltpu.make_async_copy(c_hbm, cot, local_sem.at[2]),
        pltpu.make_async_copy(w_hbm, wv, local_sem.at[3]),
    ]
    for load in loads:
        load.start()

    barrier = pltpu.get_barrier_semaphore()
    for axis in ("core", "x", "z", "y", "l"):
        for d in distances(axis):
            pl.semaphore_signal(barrier, inc=1, device_id=peer(axis, d), device_id_type=pl.DeviceIdType.MESH)

    row = iota((128, 256), 0)
    col = iota((128, 256), 1)
    turn = ((lax.rem(row, 16) * lax.rem(col, 64)) - 16 * (row // 64)) & 63
    base = jnp.cos(turn.astype(F32) * (TWO_PI / 64))
    hi, lo = split(jnp.where(lax.rem(row // 16, 4) == col // 64, base, 0.0))
    d1[0], d1[1] = hi, lo

    row = iota((256, 256), 0)
    col = iota((256, 256), 1)
    owner = row // 8
    j = 2 * (lax.rem(owner // 4, 4) * 8 + lax.rem(owner, 4) * 2 + owner // 16) + lax.rem(row // 2, 2)
    freq = jnp.where(j >= 32, j - 64, j)
    turn = (freq * (sp * X + lax.rem(col, 128)) + 1024 * (lax.rem(row, 2) + col // 128)) & 4095
    table = jnp.cos(turn.astype(F32) * (TWO_PI / NX))
    turned = table.T
    for q in range(2):
        hi, lo = split(jnp.where(lax.rem(row // 4, 2) == q, table, 0.0))
        d2[q, 0], d2[q, 1] = hi, lo
        hi, lo = split(jnp.where(lax.rem(col // 4, 2) == q, turned, 0.0))
        d3[q, 0], d3[q, 1] = hi, lo

    pl.semaphore_wait(barrier, 13)

    count = [0]
    sends = []

    def start(src, dst, axis, d):
        n = count[0]
        count[0] += 1
        copy = pltpu.make_async_remote_copy(
            src_ref=src, dst_ref=dst, send_sem=send_sem.at[n], recv_sem=recv_sem.at[n],
            device_id=peer(axis, d), device_id_type=pl.DeviceIdType.MESH,
        )
        copy.start()
        sends.append(copy)
        return n

    def arrived(n, dst):
        pltpu.make_async_remote_copy(
            src_ref=dst, dst_ref=dst, send_sem=send_sem.at[n], recv_sem=recv_sem.at[n],
            device_id=peer("core", 1), device_id_type=pl.DeviceIdType.MESH,
        ).wait_recv()

    def forward(s, wide, chain):
        def block(n, carry):
            if wide:
                v = gp[s, pl.ds(4 * n, 4)].reshape(256, 128)
                vh, vl = split(v)
                out = dot(d1[0], vh) + (dot(d1[1], vh) + dot(d1[0], vl))
            else:
                v = u[s, pl.ds(4 * n, 4)].reshape(256, 128)
                out = dot(d1[0], v) + dot(d1[1], v)
            hi, lo = split(out)
            ab[s, 0, n, :, 0:128] = hi[:64]
            ab[s, 0, n, :, 128:256] = hi[64:]
            ab[s, 1, n, :, 0:128] = lo[:64]
            ab[s, 1, n, :, 128:256] = lo[64:]
            return carry

        lax.fori_loop(0, 8, block, 0)
        total = None
        for q in range(2):
            right = tuple(ab[s, p, 4 * q:4 * q + 4].reshape(256, 256) for p in range(2))
            part = dot3((d2[q, 0], d2[q, 1]), right, NT)
            total = part if total is None else total + part
        rs0[chain] = total.reshape(2, 4, 4, 8, 256)

    def inverse(s, chain, finish):
        y = split(ag[chain].reshape(256, 256))
        for q in range(2):
            hi, lo = split(dot3((d3[q, 0], d3[q, 1]), y))
            for h in range(2):
                lanes = slice(128 * h, 128 * h + 128)
                for p, v in enumerate((hi, lo)):
                    ul[s, 2 * q + h, p, :, 0:128] = v[:128, lanes]
                    ul[s, 2 * q + h, p, :, 128:256] = v[128:, lanes]

        def block(n, carry):
            finish(n, dot3((d4[0], d4[1]), (ul[s, n, 0], ul[s, n, 1]), NT))
            return carry

        lax.fori_loop(0, 4, block, 0)

    mask16 = (lax.rem(iota((16, 256), 1), 16) == iota((16, 256), 0)).astype(F32)
    mask512 = (lax.rem(iota((16, 512), 1), 16) == iota((16, 512), 0)).astype(F32)

    def mix(s, own):
        spread = (own[:, None, :] * mask16[None]).reshape(128, 256)
        xr[s] = one_hot_product(spread, rep[...]).reshape(2, 2, 2, 16, 512)
        parts = []
        for b in range(2):
            re = jnp.zeros((16, 128), F32)
            im = jnp.zeros((16, 128), F32)
            for k in range(8):
                q, lanes = k // 4, slice(128 * (k % 4), 128 * (k % 4) + 128)
                whole = slice(128 * k, 128 * k + 128)
                x_re, x_im = xr[s, q, b, 0, :, lanes], xr[s, q, b, 1, :, lanes]
                w_re, w_im = wv[b, :, 0, whole], wv[b, :, 1, whole]
                re = re + (w_re * x_re - w_im * x_im)
                im = im + (w_re * x_im + w_im * x_re)
            parts += [re, im]
        wide = one_hot_product(jnp.concatenate(parts, axis=0), tilet[...])
        out = jnp.sum(wide.reshape(4, 16, 512) * mask512[None], axis=1)
        return jnp.concatenate([out[:, :256], out[:, 256:]], axis=0)

    def mix_back(s, own):
        spread = (own[:, None, :] * mask16[None]).reshape(128, 256)
        g = one_hot_product(spread[:64], tile[0]) + one_hot_product(spread[64:], tile[1])
        rows = [[None] * 8 for _ in range(2)]
        for b in range(2):
            g_re, g_im = g[32 * b:32 * b + 16], g[32 * b + 16:32 * b + 32]
            for k in range(8):
                q, lanes = k // 4, slice(128 * (k % 4), 128 * (k % 4) + 128)
                whole = slice(128 * k, 128 * k + 128)
                w_re, w_im = wv[b, :, 0, whole], wv[b, :, 1, whole]
                rows[b][k] = (w_re * g_re + w_im * g_im, w_re * g_im - w_im * g_re)
                x_re, x_im = xr[s, q, b, 0, :, lanes], xr[s, q, b, 1, :, lanes]
                at = (k // 2, slice(None), slice(128 * (k % 2), 128 * (k % 2) + 128))
                d_re = x_re * g_re + x_im * g_im
                d_im = x_re * g_im - x_im * g_re
                if s == 0:
                    dw[(2 * b,) + at] = d_re
                    dw[(2 * b + 1,) + at] = d_im
                else:
                    dw[(2 * b,) + at] += d_re
                    dw[(2 * b + 1,) + at] += d_im
        stacked = jnp.concatenate(
            [
                jnp.concatenate([rows[b][4 * q + k][p] for k in range(4)], axis=1)
                for q in range(2) for b in range(2) for p in range(2)
            ],
            axis=0,
        )
        wide = one_hot_product(stacked, rept[...])
        return jnp.sum(wide.reshape(8, 16, 256) * mask16[None], axis=1)

    def chain_of(s):
        for back in range(2):
            ch = 2 * s + back
            if back == 0:
                loads[s].wait()
                forward(s, False, ch)
            n = start(rs0.at[ch, 1 - core], rc0.at[ch], "core", 1)
            yield
            arrived(n, rc0.at[ch])
            rs1[ch] = rs0[ch, core] + rc0[ch]
            ns = [start(rs1.at[ch, lax.rem(xx + d, 4)], rx.at[ch, d - 1], "x", d) for d in (1, 2, 3)]
            yield
            for d in (1, 2, 3):
                arrived(ns[d - 1], rx.at[ch, d - 1])
            rs2[ch] = (rs1[ch, xx] + rx[ch, 0]) + (rx[ch, 1] + rx[ch, 2])
            ns = [start(rs2.at[ch, lax.rem(zh + d, 4)], rz.at[ch, d - 1], "z", d) for d in (1, 2, 3)]
            yield
            for d in (1, 2, 3):
                arrived(ns[d - 1], rz.at[ch, d - 1])
            own = (rs2[ch, zh] + rz[ch, 0]) + (rz[ch, 1] + rz[ch, 2])
            if back == 0:
                ag[ch, core, xx, zh] = mix(s, own * IN_SCALE) * OUT_SCALE
            else:
                ag[ch, core, xx, zh] = mix_back(s, own * OUT_SCALE) * IN_SCALE
            here = ag.at[ch, core, xx, zh]
            ns = [start(here, here, "z", d) for d in (1, 2, 3)]
            yield
            for d in (1, 2, 3):
                arrived(ns[d - 1], ag.at[ch, core, xx, lax.rem(zh + 4 - d, 4)])
            here = ag.at[ch, core, xx]
            ns = [start(here, here, "x", d) for d in (1, 2, 3)]
            yield
            for d in (1, 2, 3):
                arrived(ns[d - 1], ag.at[ch, core, lax.rem(xx + 4 - d, 4)])
            here = ag.at[ch, core]
            n = start(here, here, "core", 1)
            yield
            arrived(n, ag.at[ch, 1 - core])
            if back == 0:
                closure = step_ref[s]

                def finish(n, field):
                    rows = pl.ds(8 * n, 8)
                    p = field.reshape(8, 64, 128) + pre[s, rows]
                    sq = p * p
                    th = jnp.tanh(GELU_C * (p + 0.044715 * (sq * p)))
                    slope = 0.5 * (1.0 + th) + 0.5 * p * (1.0 - th * th) * (GELU_C * (1.0 + 3 * 0.044715 * sq))
                    live = (iota((8, 64, 128), 1) >= closure).astype(F32)
                    gp[s, rows] = cot[s, rows].astype(F32) * live * slope

                inverse(s, ch, finish)
                forward(s, True, ch + 1)
            else:

                def finish(n, field):
                    rows = pl.ds(8 * n, 8)
                    ob[s, rows] = (field.reshape(8, 64, 128) + pre[s, rows]).astype(BF16)

                inverse(s, ch, finish)
                pltpu.make_async_copy(ob.at[s], out_hbm.at[s], local_sem.at[4 + s]).start()

    def pointwise(s):
        def block(n, carry):
            v = u[s, :, pl.ds(16 * n, 16), :].astype(F32)
            for h in range(2):
                b = v[:, 8 * h:8 * h + 8].reshape(256, 128).astype(BF16)
                out = dot(k1[0], b) + dot(k1[1], b) + bcol[...]
                pre[s, :, pl.ds(16 * n + 8 * h, 8), :] = out.reshape(32, 8, 128)
            return carry

        lax.fori_loop(0, 4, block, 0)

    def point_back(s):
        def block(n, carry):
            v = u[s, :, pl.ds(16 * n, 16), :].astype(F32)
            for h in range(2):
                b = v[:, 8 * h:8 * h + 8].reshape(256, 128).astype(BF16)
                rows = pl.ds(16 * n + 8 * h, 8)
                g = gp[s, :, rows, :].reshape(256, 128)
                gs = split(g)
                pre[s, :, rows, :] = dot3((k2[0], k2[1]), gs).reshape(32, 8, 128)
                accp[...] += dot(b, gs[0], NT) + dot(b, gs[1], NT)
                accb[...] += g
            return carry

        lax.fori_loop(0, 4, block, 0)

    def later_tables():
        d4row = iota((64, 256), 0)
        d4col = iota((64, 256), 1)
        turn = ((lax.rem(d4col, 16) * d4row) - 16 * (d4col // 128)) & 63
        base = jnp.cos(turn.astype(F32) * (TWO_PI / 64))
        for c in range(8):
            hi, lo = split(jnp.where(lax.rem(d4col // 16, 8) == c, base, 0.0))
            d4[0, 64 * c:64 * c + 64] = hi
            d4[1, 64 * c:64 * c + 64] = lo
        rep[...] = (iota((256, 512), 0) // 16 == iota((256, 512), 1) // 32).astype(BF16)
        rept[...] = (iota((512, 256), 0) // 32 == iota((512, 256), 1) // 16).astype(BF16)
        for q in range(2):
            tile[q] = (iota((256, 128), 0) // 16 + 16 * q == lax.rem(iota((256, 128), 1), 32)).astype(BF16)
        tilet[...] = (lax.rem(iota((128, 512), 0), 32) == iota((128, 512), 1) // 16).astype(BF16)

    def point_tables():
        pick = (iota((256, 32), 0) // 8 == iota((256, 32), 1)).astype(F32)
        onehot[...] = pick
        e = pick.astype(BF16)
        same = lax.rem(iota((256, 256), 0), 8) == lax.rem(iota((256, 256), 1), 8)
        for p, v in enumerate(split(pw_ref[...])):
            k2[p] = jnp.where(same, dot(dot(e, v).astype(BF16), e, NT), 0.0).astype(BF16)
            k1[p] = jnp.where(same, dot(dot(e, v, NT).astype(BF16), e, NT), 0.0).astype(BF16)
        column = jnp.sum(pick * bias_ref[...], axis=1, keepdims=True)
        bcol[...] = jnp.broadcast_to(column, (256, 128))
        accp[...] = jnp.zeros((256, 256), F32)
        accb[...] = jnp.zeros((256, 128), F32)

    def small_sum():
        same = (lax.rem(iota((256, 256), 0), 8) == lax.rem(iota((256, 256), 1), 8)).astype(F32)
        by_row = dot_exact((iota((32, 256), 1) // 8 == iota((32, 256), 0)).astype(F32), accp[...] * same)
        four = (iota((256, 128), 0) // 8 == lax.rem(iota((256, 128), 1), 32)).astype(F32)
        grid = dot_exact(by_row, four)
        grid = jnp.where(lax.rem(iota((32, 128), 0), 4) == iota((32, 128), 1) // 32, grid, 0.0)
        small[0, 0:8] = dot_exact((iota((8, 32), 1) // 4 == iota((8, 32), 0)).astype(F32), grid)
        column = jnp.sum(accb[...], axis=1, keepdims=True)
        line = jnp.sum(column * four, axis=0, keepdims=True)
        small[0, 8:16] = jnp.broadcast_to(line, (8, 128))
        n = start(small.at[0], sc_, "core", 1)
        yield
        arrived(n, sc_)
        small[1] = small[0] + sc_[...]
        for k, (axis, got) in enumerate((("x", sx), ("z", sz), ("y", sy), ("l", szl))):
            ns = [start(small.at[1 + k], got.at[d - 1], axis, d) for d in (1, 2, 3)]
            yield
            for d in (1, 2, 3):
                arrived(ns[d - 1], got.at[d - 1])
            small[2 + k] = (small[1 + k] + got[0]) + (got[1] + got[2])
        total = small[5] * POINT_SCALE
        spread = dot_exact((iota((32, 8), 0) // 4 == iota((32, 8), 1)).astype(F32), total[0:8])
        spread = jnp.where(lax.rem(iota((32, 128), 0), 4) == iota((32, 128), 1) // 32, spread, 0.0)
        point_out[...] = dot_exact(spread, (lax.rem(iota((128, 32), 0), 32) == iota((128, 32), 1)).astype(F32))
        bias_out[...] = total[8:9, 0:32]

    def weight_sum():
        ns = [start(dw.at[lax.rem(yy + d, 4)], ry.at[d - 1], "y", d) for d in (1, 2, 3)]
        yield
        for d in (1, 2, 3):
            arrived(ns[d - 1], ry.at[d - 1])
        dw1[...] = (dw[yy] + ry[0]) + (ry[1] + ry[2])
        ns = [start(dw1.at[lax.rem(zl + d, 4)], rzl.at[d - 1], "l", d) for d in (1, 2, 3)]
        yield
        for d in (1, 2, 3):
            arrived(ns[d - 1], rzl.at[d - 1])
        dwf[yy, zl] = ((dw1[zl] + rzl[0]) + (rzl[1] + rzl[2])) * SAMPLE_SCALE
        here = dwf.at[yy, zl]
        ns = [start(here, here, "l", d) for d in (1, 2, 3)]
        yield
        for d in (1, 2, 3):
            arrived(ns[d - 1], dwf.at[yy, lax.rem(zl + 4 - d, 4)])
        here = dwf.at[yy]
        ns = [start(here, here, "y", d) for d in (1, 2, 3)]
        yield
        for d in (1, 2, 3):
            arrived(ns[d - 1], dwf.at[lax.rem(yy + 4 - d, 4)])
        pltpu.make_async_copy(dwf, dw_out, local_sem.at[6]).start()

    a, b = chain_of(0), chain_of(1)
    smalls, weights = small_sum(), weight_sum()

    def go(*parts):
        for part in parts:
            next(part, None)

    go(a, b)
    later_tables()
    point_tables()
    go(a, b)
    pointwise(0)
    go(a, b)
    loads[3].wait()
    go(a, b)
    pointwise(1)
    go(a, b)
    go(a, b)
    loads[2].wait()
    go(a, b)
    point_back(0)
    go(a, b)
    point_back(1)
    go(smalls)
    go(a, b)
    go(smalls)
    go(a, b)
    go(weights, smalls)
    go(a, b)
    go(weights, smalls)
    go(a, b)
    go(weights, smalls)
    go(a)
    go(weights, smalls)
    go(b)
    go(weights)

    for copy in sends:
        copy.wait_send()
    pltpu.make_async_copy(ob.at[0], out_hbm.at[0], local_sem.at[4]).wait()
    pltpu.make_async_copy(ob.at[1], out_hbm.at[1], local_sem.at[5]).wait()
    pltpu.make_async_copy(dwf, dw_out, local_sem.at[6]).wait()


COPIES = 4 * 14 + 13 + 12


def body(layer_input, cotangent, closure_step, spectral_weight, point_weight, bias):
    anywhere = pl.BlockSpec(memory_space=pl.ANY)
    vmem = pl.BlockSpec(memory_space=pltpu.VMEM)
    V = pltpu.VMEM
    scratch = [
        V((S, C, T, X), BF16), V((S, C, T, X), BF16), V((2, 16, 2, 1024), F32),
        V((S, C, T, X), F32), V((S, C, T, X), F32), V((S, C, T, X), BF16),
        V((2, 128, 256), BF16), V((2, 2, 256, 256), BF16), V((2, 2, 256, 256), BF16), V((2, 512, 256), BF16),
        V((2, 256, 256), BF16), V((2, 256, 256), BF16),
        V((256, 512), BF16), V((512, 256), BF16), V((2, 256, 128), BF16), V((128, 512), BF16),
        V((256, 128), F32), V((256, 32), F32),
        V((S, 2, 8, 64, 256), BF16), V((S, 4, 2, 128, 256), BF16), V((S, 2, 2, 2, 16, 512), F32),
        V((256, 256), F32), V((256, 128), F32),
        V((4, 2, 4, 4, 8, 256), F32), V((4, 4, 4, 8, 256), F32), V((4, 4, 4, 8, 256), F32),
        V((4, 3, 4, 8, 256), F32), V((4, 4, 8, 256), F32), V((4, 3, 8, 256), F32), V((4, 2, 4, 4, 8, 256), F32),
        V((4, 4, 16, 256), F32), V((3, 4, 16, 256), F32), V((4, 16, 256), F32), V((3, 16, 256), F32),
        V((4, 4, 16, 256), F32),
        V((6, 16, 128), F32), V((16, 128), F32), V((3, 16, 128), F32), V((3, 16, 128), F32),
        V((3, 16, 128), F32), V((3, 16, 128), F32),
        pltpu.SemaphoreType.DMA((7,)), pltpu.SemaphoreType.DMA((COPIES,)), pltpu.SemaphoreType.DMA((COPIES,)),
    ]
    grad, dw, point, bias_grad = pl.pallas_call(
        kernel,
        out_shape=(
            jax.ShapeDtypeStruct((S, C, T, X), BF16),
            jax.ShapeDtypeStruct((4, 4, 16, 256), F32),
            jax.ShapeDtypeStruct((C, C), F32),
            jax.ShapeDtypeStruct((1, C), F32),
        ),
        in_specs=[anywhere, anywhere, pl.BlockSpec(memory_space=pltpu.SMEM), anywhere, vmem, vmem],
        out_specs=(anywhere, anywhere, vmem, vmem),
        scratch_shapes=scratch,
        compiler_params=pltpu.CompilerParams(
            collective_id=0, has_side_effects=True, vmem_limit_bytes=48 * 1024 * 1024
        ),
    )(layer_input, cotangent, closure_step, spectral_weight, point_weight, bias.reshape(1, C))
    dw = dw.reshape(2, 2, 4, 16, 256).transpose(0, 3, 1, 2, 4).reshape(2, 16, 2, 1024)
    return grad, dw, point, bias_grad.reshape(C)


def solution(mesh):
    return jax.shard_map(
        body,
        mesh=mesh,
        in_specs=(
            P("dp", None, None, "space"),
            P("dp", None, None, "space"),
            P("dp"),
            P("space", None, None, None),
            P(),
            P(),
        ),
        out_specs=(P("dp", None, None, "space"), P("space", None, None, None), P(), P()),
        check_vma=False,
    )
```

```python
import functools
import math

import jax
import jax.numpy as jnp
from jax import lax
from jax.experimental import pallas as pl
from jax.experimental.pallas import tpu as pltpu
from jax.sharding import PartitionSpec as P

F32 = jnp.float32
BF16 = jnp.bfloat16
S, C, T, X, M = 2, 32, 64, 128, 16
GROUPS = 32
NX = X * GROUPS
NN = (((1,), (0,)), ((), ()))
NT = (((1,), (1,)), ((), ()))
TWO_PI = 2.0 * math.pi
POINT_SCALE = 1.0 / math.sqrt(32 * T * NX)
SAMPLE_SCALE = 1.0 / math.sqrt(32)
IN_SCALE = 1.0 / 512.0
OUT_SCALE = 1.0 / 32.0
GELU_C = math.sqrt(2.0 / math.pi)


def iota(shape, axis):
    return lax.broadcasted_iota(jnp.int32, shape, axis)


def wave(turn):
    near = turn + 512
    t = ((near & 1023) - 512).astype(F32) * (TWO_PI / NX)
    quarter = (near >> 10) & 3
    sq = t * t
    even = 1.0 + sq * (-1 / 2 + sq * (1 / 24 + sq * (-1 / 720 + sq * (1 / 40320))))
    odd = t * (1.0 + sq * (-1 / 6 + sq * (1 / 120 + sq * (-1 / 5040 + sq * (1 / 362880)))))
    value = jnp.where((quarter & 1) == 0, even, odd)
    return jnp.where(((quarter + 1) & 2) == 0, value, -value)


def split(v):
    hi = v.astype(BF16)
    return hi, (v - hi.astype(F32)).astype(BF16)


def dot(a, b, dims=NN):
    return lax.dot_general(a, b, dims, preferred_element_type=F32)


def dot3(a, b, dims=NN):
    return dot(a[0], b[0], dims) + (dot(a[0], b[1], dims) + dot(a[1], b[0], dims))


def dot_exact(a, b, dims=NN):
    return lax.dot_general(a, b, dims, preferred_element_type=F32, precision=lax.Precision.HIGHEST)


def one_hot_product(rows, table):
    hi, lo = split(rows)
    n = rows.shape[0]
    both = dot(jnp.concatenate([hi, lo], axis=0), table)
    return both[:n] + both[n:]


def kernel(
    u_hbm, c_hbm, step_ref, w_hbm, pw_ref, bias_ref,
    out_hbm, dw_out, point_out, bias_out,
    u, cot, wv, pw, bv, pre, gp, ob,
    d1, d2, d3, d4, k1, k2, rep, rept, tile, tilet, bcol, onehot,
    ab, ul, xr, accp, accb,
    rs0, rcx, rs1, rz, mine, ag,
    dw, ry, dw1, rzl, dwf,
    small, scx, sz, sy, szl,
    local_sem, send_sem, recv_sem,
):
    dp = lax.axis_index("dp")
    sp = lax.axis_index("space")
    core = lax.rem(sp, 2)
    zh = lax.rem(sp // 2, 4)
    xx = sp // 8
    yy = dp // 4
    zl = lax.rem(dp, 4)

    def device(x=xx, z=zh, c=core, y=yy, l=zl):
        return (y * 4 + l, x * 8 + z * 2 + c)

    zl2 = lax.rem(zl + 2, 4)
    first = jnp.where(zl < 2, 1, 2)
    others = [(0, 1), (0, 2), (0, 3), (1, 0), (1, 1), (1, 2), (1, 3)]

    def plane(dc, d):
        return device(x=lax.rem(xx + d, 4), c=lax.rem(core + dc, 2))

    def owner_of(i):
        return device(z=lax.rem(zh + first + i, 4), l=zl2)

    def served(i):
        return device(z=lax.rem(zh + first + 5 - i, 4), l=zl2)

    def peer(axis, d):
        if axis == "y":
            return device(y=lax.rem(yy + d, 4))
        return device(l=lax.rem(zl + d, 4))

    loads = [
        pltpu.make_async_copy(u_hbm.at[0], u.at[0], local_sem.at[0]),
        pltpu.make_async_copy(u_hbm.at[1], u.at[1], local_sem.at[1]),
        pltpu.make_async_copy(c_hbm, cot, local_sem.at[2]),
        pltpu.make_async_copy(w_hbm, wv, local_sem.at[3]),
        pltpu.make_async_copy(pw_ref, pw, local_sem.at[7]),
        pltpu.make_async_copy(bias_ref, bv, local_sem.at[8]),
    ]
    for load in loads:
        load.start()

    barrier = pltpu.get_barrier_semaphore()
    greeted = [plane(*o) for o in others] + [owner_of(i) for i in range(4)]
    greeted += [peer(axis, d) for axis in ("y", "l") for d in (1, 2, 3)]
    for who in greeted:
        pl.semaphore_signal(barrier, inc=1, device_id=who, device_id_type=pl.DeviceIdType.MESH)

    row = iota((128, 256), 0)
    col = iota((128, 256), 1)
    base = wave((((row & 15) * (col & 63)) - 16 * (row >> 6)) * 64)
    hi, lo = split(jnp.where(((row >> 4) & 3) == (col >> 6), base, 0.0))
    d1[0:128], d1[128:256] = hi, lo

    row = iota((256, 256), 0)
    col = iota((256, 256), 1)
    owner = row >> 3
    owner_z = (zh + first + 2 * (owner >> 4) + (owner & 1)) & 3
    j = 2 * (((owner >> 1) & 3) * 8 + owner_z * 2 + ((owner >> 3) & 1)) + ((row >> 1) & 1)
    freq = jnp.where(j >= 32, j - 64, j)
    table = wave(freq * (sp * X + (col & 127)) + 1024 * ((row & 1) + (col >> 7)))
    turned = table.T
    for q in range(2):
        hi, lo = split(jnp.where(((row >> 2) & 1) == q, table, 0.0))
        d2[q, 0], d2[q, 1] = hi, lo
        hi, lo = split(jnp.where(((col >> 2) & 1) == q, turned, 0.0))
        d3[q, 0], d3[q, 1] = hi, lo

    count = [0]
    sends = []

    def start(src, dst, who):
        n = count[0]
        count[0] += 1
        copy = pltpu.make_async_remote_copy(
            src_ref=src, dst_ref=dst, send_sem=send_sem.at[n], recv_sem=recv_sem.at[n],
            device_id=who, device_id_type=pl.DeviceIdType.MESH,
        )
        copy.start()
        sends.append(copy)
        return n

    def arrived(n, dst):
        pltpu.make_async_remote_copy(
            src_ref=dst, dst_ref=dst, send_sem=send_sem.at[n], recv_sem=recv_sem.at[n],
            device_id=plane(1, 0), device_id_type=pl.DeviceIdType.MESH,
        ).wait_recv()

    def forward(s, wide, chain):
        def block(n, carry):
            if wide:
                v = jnp.concatenate(split(gp[s, pl.ds(4 * n, 4)].reshape(256, 128)), axis=1)
                both = dot(d1[...], v)
                out = both[:128, :128] + (both[128:, :128] + both[:128, 128:])
            else:
                both = dot(d1[...], u[s, pl.ds(4 * n, 4)].reshape(256, 128))
                out = both[:128] + both[128:]
            hi, lo = split(out)
            ab[s, 0, n, :, 0:128] = hi[:64]
            ab[s, 0, n, :, 128:256] = hi[64:]
            ab[s, 1, n, :, 0:128] = lo[:64]
            ab[s, 1, n, :, 128:256] = lo[64:]
            return carry

        lax.fori_loop(0, 8, block, 0)
        total = None
        for q in range(2):
            right = tuple(ab[s, p, 4 * q:4 * q + 4].reshape(256, 256) for p in range(2))
            part = dot3((d2[q, 0], d2[q, 1]), right, NT)
            total = part if total is None else total + part
        rs0[chain] = total.reshape(2, 2, 4, 2, 8, 256)

    def inverse(s, chain, finish):
        y = split(ag[chain].reshape(256, 256))
        for q in range(2):
            hi, lo = split(dot3((d3[q, 0], d3[q, 1]), y))
            for h in range(2):
                lanes = slice(128 * h, 128 * h + 128)
                for p, v in enumerate((hi, lo)):
                    ul[s, 2 * q + h, 128 * p:128 * p + 128, 0:128] = v[:128, lanes]
                    ul[s, 2 * q + h, 128 * p:128 * p + 128, 128:256] = v[128:, lanes]

        def block(n, carry):
            both = dot(d4[0], ul[s, n], NT)
            finish(n, both[:, :128] + (both[:, 128:] + dot(d4[1], ul[s, n, 0:128], NT)))
            return carry

        lax.fori_loop(0, 4, block, 0)

    mask16 = ((iota((16, 256), 1) & 15) == iota((16, 256), 0)).astype(F32)
    mask512 = ((iota((16, 512), 1) & 15) == iota((16, 512), 0)).astype(F32)

    def mix(s, own):
        spread = (own[:, None, :] * mask16[None]).reshape(128, 256)
        xr[s] = one_hot_product(spread, rep[...]).reshape(2, 2, 2, 16, 512)
        parts = []
        for b in range(2):
            re = jnp.zeros((16, 128), F32)
            im = jnp.zeros((16, 128), F32)
            for k in range(8):
                q, lanes = k // 4, slice(128 * (k % 4), 128 * (k % 4) + 128)
                whole = slice(128 * k, 128 * k + 128)
                x_re, x_im = xr[s, q, b, 0, :, lanes], xr[s, q, b, 1, :, lanes]
                w_re, w_im = wv[b, :, 0, whole], wv[b, :, 1, whole]
                re = re + (w_re * x_re - w_im * x_im)
                im = im + (w_re * x_im + w_im * x_re)
            parts += [re, im]
        wide = one_hot_product(jnp.concatenate(parts, axis=0), tilet[...])
        out = jnp.sum(wide.reshape(4, 16, 512) * mask512[None], axis=1)
        return jnp.concatenate([out[:, :256], out[:, 256:]], axis=0)

    def mix_back(s, own, after):
        spread = (own[:, None, :] * mask16[None]).reshape(128, 256)
        g = one_hot_product(spread[:64], tile[0]) + one_hot_product(spread[64:], tile[1])
        gs = [(g[32 * b:32 * b + 16], g[32 * b + 16:32 * b + 32]) for b in range(2)]
        for b in range(2):
            g_re, g_im = gs[b]
            for k in range(8):
                q, lanes = k // 4, slice(128 * (k % 4), 128 * (k % 4) + 128)
                x_re, x_im = xr[s, q, b, 0, :, lanes], xr[s, q, b, 1, :, lanes]
                at = (k // 2, slice(None), slice(128 * (k % 2), 128 * (k % 2) + 128))
                d_re = x_re * g_re + x_im * g_im
                d_im = x_re * g_im - x_im * g_re
                if s == 0:
                    dw[(2 * b,) + at] = d_re
                    dw[(2 * b + 1,) + at] = d_im
                else:
                    dw[(2 * b,) + at] += d_re
                    dw[(2 * b + 1,) + at] += d_im
        after()
        rows = [[None] * 8 for _ in range(2)]
        for b in range(2):
            g_re, g_im = gs[b]
            for k in range(8):
                whole = slice(128 * k, 128 * k + 128)
                w_re, w_im = wv[b, :, 0, whole], wv[b, :, 1, whole]
                rows[b][k] = (w_re * g_re + w_im * g_im, w_re * g_im - w_im * g_re)
        stacked = jnp.concatenate(
            [
                jnp.concatenate([rows[b][4 * q + k][p] for k in range(4)], axis=1)
                for q in range(2) for b in range(2) for p in range(2)
            ],
            axis=0,
        )
        wide = one_hot_product(stacked, rept[...])
        return jnp.sum(wide.reshape(8, 16, 256) * mask16[None], axis=1)

    def chain_of(s):
        for back in range(2):
            ch = 2 * s + back
            if back == 0:
                loads[s].wait()
                forward(s, False, ch)
                yield
            ns = [
                [start(rs0.at[ch, far, lax.rem(core + dc, 2), lax.rem(xx + d, 4)], rcx.at[ch, far, p], plane(dc, d))
                 for p, (dc, d) in enumerate(others)]
                for far in range(2)
            ]
            yield
            zs = []
            for far in range(2):
                total = rs0[ch, far, core, xx]
                for p in range(7):
                    arrived(ns[far][p], rcx.at[ch, far, p])
                    total = total + rcx[ch, far, p]
                rs1[ch, far] = total
                zs += [start(rs1.at[ch, far, k], rz.at[ch, 2 * far + k], owner_of(2 * far + k)) for k in range(2)]
                yield
            for i in (2, 3, 0, 1):
                arrived(zs[i], rz.at[ch, i])
            own = (rz[ch, 0] + rz[ch, 1]) + (rz[ch, 2] + rz[ch, 3])
            if back == 0:
                mine[ch] = mix(s, own * IN_SCALE) * OUT_SCALE
            else:
                mine[ch] = mix_back(s, own * OUT_SCALE, lambda: next(weights) if s == 1 else None) * IN_SCALE
            zs = [start(mine.at[ch], ag.at[ch, i // 2, core, xx, i % 2], served(i)) for i in range(4)]
            yield
            ns = [None, None]
            for far in (1, 0):
                for k in range(2):
                    arrived(zs[2 * far + k], ag.at[ch, far, core, xx, k])
                here = ag.at[ch, far, core, xx]
                ns[far] = [start(here, here, plane(dc, d)) for dc, d in others]
                yield
            for far in (1, 0):
                for p, (dc, d) in enumerate(others):
                    arrived(ns[far][p], ag.at[ch, far, lax.rem(core + dc, 2), lax.rem(xx + 4 - d, 4)])
            if back == 0:
                closure = step_ref[s]

                def finish(n, field):
                    rows = pl.ds(8 * n, 8)
                    p = field.reshape(8, 64, 128) + pre[s, rows]
                    sq = p * p
                    th = jnp.tanh(GELU_C * (p + 0.044715 * (sq * p)))
                    slope = 0.5 * (1.0 + th) + 0.5 * p * (1.0 - th * th) * (GELU_C * (1.0 + 3 * 0.044715 * sq))
                    live = (iota((8, 64, 128), 1) >= closure).astype(F32)
                    gp[s, rows] = cot[s, rows].astype(F32) * live * slope

                inverse(s, ch, finish)
                forward(s, True, ch + 1)
            else:

                def finish(n, field):
                    rows = pl.ds(8 * n, 8)
                    ob[s, rows] = (field.reshape(8, 64, 128) + pre[s, rows]).astype(BF16)

                inverse(s, ch, finish)
                pltpu.make_async_copy(ob.at[s], out_hbm.at[s], local_sem.at[4 + s]).start()

    def pointwise(s):
        def block(n, carry):
            v = u[s, :, pl.ds(16 * n, 16), :].astype(F32)
            for h in range(2):
                b = v[:, 8 * h:8 * h + 8].reshape(256, 128).astype(BF16)
                out = dot(k1[0], b) + dot(k1[1], b) + bcol[...]
                pre[s, :, pl.ds(16 * n + 8 * h, 8), :] = out.reshape(32, 8, 128)
            return carry

        lax.fori_loop(0, 4, block, 0)

    def point_back(s):
        def block(n, carry):
            v = u[s, :, pl.ds(16 * n, 16), :].astype(F32)
            for h in range(2):
                b = v[:, 8 * h:8 * h + 8].reshape(256, 128).astype(BF16)
                rows = pl.ds(16 * n + 8 * h, 8)
                g = gp[s, :, rows, :].reshape(256, 128)
                gs = split(g)
                pre[s, :, rows, :] = dot3((k2[0], k2[1]), gs).reshape(32, 8, 128)
                accp[...] += dot(b, gs[0], NT) + dot(b, gs[1], NT)
                accb[...] += g
            return carry

        lax.fori_loop(0, 4, block, 0)

    def later_tables():
        d4row = iota((64, 256), 0)
        d4col = iota((64, 256), 1)
        base = wave((((d4col & 15) * d4row) - 16 * (d4col >> 7)) * 64)
        for c in range(8):
            hi, lo = split(jnp.where(((d4col >> 4) & 7) == c, base, 0.0))
            d4[0, 64 * c:64 * c + 64] = hi
            d4[1, 64 * c:64 * c + 64] = lo
        rep[...] = ((iota((256, 512), 0) >> 4) == (iota((256, 512), 1) >> 5)).astype(BF16)
        rept[...] = ((iota((512, 256), 0) >> 5) == (iota((512, 256), 1) >> 4)).astype(BF16)
        for q in range(2):
            tile[q] = ((iota((256, 128), 0) >> 4) + 16 * q == (iota((256, 128), 1) & 31)).astype(BF16)
        tilet[...] = ((iota((128, 512), 0) & 31) == (iota((128, 512), 1) >> 4)).astype(BF16)

    def point_tables():
        pick = ((iota((256, 32), 0) >> 3) == iota((256, 32), 1)).astype(F32)
        onehot[...] = pick
        e = pick.astype(BF16)
        same = (iota((256, 256), 0) & 7) == (iota((256, 256), 1) & 7)
        for p, v in enumerate(split(pw[...])):
            k2[p] = jnp.where(same, dot(dot(e, v).astype(BF16), e, NT), 0.0).astype(BF16)
            k1[p] = jnp.where(same, dot(dot(e, v, NT).astype(BF16), e, NT), 0.0).astype(BF16)
        column = jnp.sum(pick * bv[...], axis=1, keepdims=True)
        bcol[...] = jnp.broadcast_to(column, (256, 128))
        accp[...] = jnp.zeros((256, 256), F32)
        accb[...] = jnp.zeros((256, 128), F32)

    def small_sum():
        same = ((iota((256, 256), 0) & 7) == (iota((256, 256), 1) & 7)).astype(F32)
        by_row = dot_exact(((iota((32, 256), 1) >> 3) == iota((32, 256), 0)).astype(F32), accp[...] * same)
        four = ((iota((256, 128), 0) >> 3) == (iota((256, 128), 1) & 31)).astype(F32)
        grid = dot_exact(by_row, four)
        grid = jnp.where((iota((32, 128), 0) & 3) == (iota((32, 128), 1) >> 5), grid, 0.0)
        small[0, 0:8] = dot_exact(((iota((8, 32), 1) >> 2) == iota((8, 32), 0)).astype(F32), grid)
        column = jnp.sum(accb[...], axis=1, keepdims=True)
        line = jnp.sum(column * four, axis=0, keepdims=True)
        small[0, 8:16] = jnp.broadcast_to(line, (8, 128))
        ns = [start(small.at[0], scx.at[p], plane(*o)) for p, o in enumerate(others)]
        yield
        total = small[0]
        for p in range(7):
            arrived(ns[p], scx.at[p])
            total = total + scx[p]
        small[1] = total
        ns = [start(small.at[1], sz.at[i], owner_of(i)) for i in range(4)]
        yield
        for i in range(4):
            arrived(ns[i], sz.at[i])
        small[2] = (sz[0] + sz[1]) + (sz[2] + sz[3])
        for k, (axis, got) in enumerate((("y", sy), ("l", szl))):
            ns = [start(small.at[2 + k], got.at[d - 1], peer(axis, d)) for d in (1, 2, 3)]
            yield
            for d in (1, 2, 3):
                arrived(ns[d - 1], got.at[d - 1])
            small[3 + k] = (small[2 + k] + got[0]) + (got[1] + got[2])
        total = small[4] * POINT_SCALE
        spread = dot_exact(((iota((32, 8), 0) >> 2) == iota((32, 8), 1)).astype(F32), total[0:8])
        spread = jnp.where((iota((32, 128), 0) & 3) == (iota((32, 128), 1) >> 5), spread, 0.0)
        point_out[...] = dot_exact(spread, ((iota((128, 32), 0) & 31) == iota((128, 32), 1)).astype(F32))
        bias_out[...] = total[8:9, 0:32]

    def weight_sum():
        near = [lax.rem(zl + d, 4) for d in range(4)]
        ns = {
            d: [start(dw.at[lax.rem(yy + e, 4), near[d]], ry.at[e - 1, d], peer("y", e)) for e in (1, 2, 3)]
            for d in (2, 1, 3, 0)
        }
        yield
        zs = {}
        for d in (2, 1, 3, 0):
            for e in (1, 2, 3):
                arrived(ns[d][e - 1], ry.at[e - 1, d])
            dw1[d] = (dw[yy, near[d]] + ry[0, d]) + (ry[1, d] + ry[2, d])
            if d > 0:
                zs[d] = start(dw1.at[d], rzl.at[d - 1], peer("l", d))
        yield
        for d in (1, 2, 3):
            arrived(zs[d], rzl.at[d - 1])
        dwf[yy, zl] = ((dw1[0] + rzl[0]) + (rzl[1] + rzl[2])) * SAMPLE_SCALE
        here = dwf.at[yy, zl]
        zs = {d: start(here, here, peer("l", d)) for d in (2, 1, 3)}
        ns = {0: [start(here, here, peer("y", e)) for e in (1, 2, 3)]}
        yield
        for d in (1, 3, 2):
            here = dwf.at[yy, lax.rem(zl + 4 - d, 4)]
            arrived(zs[d], here)
            ns[d] = [start(here, here, peer("y", e)) for e in (1, 2, 3)]
        yield
        for d in (0, 1, 3, 2):
            for e in (1, 2, 3):
                arrived(ns[d][e - 1], dwf.at[lax.rem(yy + 4 - e, 4), lax.rem(zl + 4 - d, 4)])
        pltpu.make_async_copy(dwf, dw_out, local_sem.at[6]).start()

    a, b = chain_of(0), chain_of(1)
    smalls, weights = small_sum(), weight_sum()

    def go(*parts):
        for part in parts:
            next(part, None)

    go(a, b)
    loads[4].wait()
    loads[5].wait()
    point_tables()
    pl.semaphore_wait(barrier, len(greeted))
    go(a, b)
    later_tables()
    go(a, a, b, b)
    pointwise(0)
    pointwise(1)
    loads[3].wait()
    go(a, b)
    go(a, b)
    go(a, b)
    loads[2].wait()
    go(a)
    go(b)
    point_back(0)
    go(a, a, b, b)
    point_back(1)
    go(smalls)
    go(a, b)
    go(smalls)
    go(weights)
    go(a, b)
    go(a, b)
    go(weights)
    go(smalls)
    go(a)
    go(weights)
    go(smalls)
    go(b)
    go(smalls)
    go(weights)

    for copy in sends:
        copy.wait_send()
    pltpu.make_async_copy(ob.at[0], out_hbm.at[0], local_sem.at[4]).wait()
    pltpu.make_async_copy(ob.at[1], out_hbm.at[1], local_sem.at[5]).wait()
    pltpu.make_async_copy(dwf, dw_out, local_sem.at[6]).wait()


def place(grad, dw, point, bias, out, dw_out, point_out, bias_out, held, piece, whole, sem):
    loads = [pltpu.make_async_copy(grad.at[s], held.at[s], sem.at[s]) for s in range(2)]
    stores = [pltpu.make_async_copy(held.at[s], out.at[s], sem.at[2 + s]) for s in range(2)]
    load = pltpu.make_async_copy(dw, piece, sem.at[4])
    store = pltpu.make_async_copy(whole, dw_out, sem.at[5])
    load.start()
    for copy in loads:
        copy.start()
    point_out[...] = point[...]
    bias_out[...] = bias[...]
    load.wait()
    for b in range(2):
        for p in range(2):
            for q in range(4):
                whole[b, :, p, 256 * q:256 * q + 256] = piece[2 * b + p, q]
    store.start()
    for s in range(2):
        loads[s].wait()
        stores[s].start()
    for copy in [store] + stores:
        copy.wait()


COPIES = 4 * 36 + 17 + 30


def body(layer_input, cotangent, closure_step, spectral_weight, point_weight, bias):
    anywhere = pl.BlockSpec(memory_space=pl.ANY)
    vmem = pl.BlockSpec(memory_space=pltpu.VMEM)
    V = pltpu.VMEM
    scratch = [
        V((S, C, T, X), BF16), V((S, C, T, X), BF16), V((2, 16, 2, 1024), F32), V((C, C), F32), V((1, C), F32),
        V((S, C, T, X), F32), V((S, C, T, X), F32), V((S, C, T, X), BF16),
        V((256, 256), BF16), V((2, 2, 256, 256), BF16), V((2, 2, 256, 256), BF16), V((2, 512, 256), BF16),
        V((2, 256, 256), BF16), V((2, 256, 256), BF16),
        V((256, 512), BF16), V((512, 256), BF16), V((2, 256, 128), BF16), V((128, 512), BF16),
        V((256, 128), F32), V((256, 32), F32),
        V((S, 2, 8, 64, 256), BF16), V((S, 4, 256, 256), BF16), V((S, 2, 2, 2, 16, 512), F32),
        V((256, 256), F32), V((256, 128), F32),
        V((4, 2, 2, 4, 2, 8, 256), F32), V((4, 2, 7, 2, 8, 256), F32), V((4, 2, 2, 8, 256), F32),
        V((4, 4, 8, 256), F32), V((4, 8, 256), F32), V((4, 2, 2, 4, 2, 8, 256), F32),
        V((4, 4, 16, 256), F32), V((3, 4, 16, 256), F32), V((4, 16, 256), F32), V((3, 16, 256), F32),
        V((4, 4, 16, 256), F32),
        V((5, 16, 128), F32), V((7, 16, 128), F32), V((4, 16, 128), F32), V((3, 16, 128), F32), V((3, 16, 128), F32),
        pltpu.SemaphoreType.DMA((9,)), pltpu.SemaphoreType.DMA((COPIES,)), pltpu.SemaphoreType.DMA((COPIES,)),
    ]
    grad, dw, point, bias_grad = pl.pallas_call(
        kernel,
        out_shape=(
            jax.ShapeDtypeStruct((S, C, T, X), BF16),
            jax.ShapeDtypeStruct((4, 4, 16, 256), F32),
            jax.ShapeDtypeStruct((C, C), F32),
            jax.ShapeDtypeStruct((1, C), F32),
        ),
        in_specs=[anywhere, anywhere, pl.BlockSpec(memory_space=pltpu.SMEM), anywhere, anywhere, anywhere],
        out_specs=(anywhere, anywhere, vmem, vmem),
        scratch_shapes=scratch,
        compiler_params=pltpu.CompilerParams(
            collective_id=0, has_side_effects=True, vmem_limit_bytes=60 * 1024 * 1024
        ),
    )(layer_input, cotangent, closure_step, spectral_weight, point_weight, bias.reshape(1, C))
    grad, dw, point, bias_grad = pl.pallas_call(
        place,
        out_shape=(
            jax.ShapeDtypeStruct((S, C, T, X), BF16),
            jax.ShapeDtypeStruct((2, 16, 2, 1024), F32),
            jax.ShapeDtypeStruct((C, C), F32),
            jax.ShapeDtypeStruct((1, C), F32),
        ),
        in_specs=[anywhere, anywhere, vmem, vmem],
        out_specs=(anywhere, anywhere, vmem, vmem),
        scratch_shapes=[
            V((S, C, T, X), BF16), V((4, 4, 16, 256), F32), V((2, 16, 2, 1024), F32), pltpu.SemaphoreType.DMA((6,)),
        ],
        compiler_params=pltpu.CompilerParams(vmem_limit_bytes=60 * 1024 * 1024),
    )(grad, dw, point, bias_grad)
    return grad, dw, point, bias_grad.reshape(C)


def solution(mesh):
    return jax.shard_map(
        body,
        mesh=mesh,
        in_specs=(
            P("dp", None, None, "space"),
            P("dp", None, None, "space"),
            P("dp"),
            P("space", None, None, None),
            P(),
            P(),
        ),
        out_specs=(P("dp", None, None, "space"), P("space", None, None, None), P(), P()),
        check_vma=False,
    )
```

```python
import functools
import math

import jax
import jax.numpy as jnp
from jax import lax
from jax.experimental import pallas as pl
from jax.experimental.pallas import tpu as pltpu
from jax.sharding import PartitionSpec as P

F32 = jnp.float32
BF16 = jnp.bfloat16
S, C, T, X, M = 2, 32, 64, 128, 16
GROUPS = 32
NX = X * GROUPS
NN = (((1,), (0,)), ((), ()))
NT = (((1,), (1,)), ((), ()))
TWO_PI = 2.0 * math.pi
POINT_SCALE = 1.0 / math.sqrt(32 * T * NX)
SAMPLE_SCALE = 1.0 / math.sqrt(32)
IN_SCALE = 1.0 / 512.0
OUT_SCALE = 1.0 / 32.0
GELU_C = math.sqrt(2.0 / math.pi)


def iota(shape, axis):
    return lax.broadcasted_iota(jnp.int32, shape, axis)


def wave(turn):
    near = turn + 512
    t = ((near & 1023) - 512).astype(F32) * (TWO_PI / NX)
    quarter = (near >> 10) & 3
    sq = t * t
    even = 1.0 + sq * (-1 / 2 + sq * (1 / 24 + sq * (-1 / 720 + sq * (1 / 40320))))
    odd = t * (1.0 + sq * (-1 / 6 + sq * (1 / 120 + sq * (-1 / 5040 + sq * (1 / 362880)))))
    value = jnp.where((quarter & 1) == 0, even, odd)
    return jnp.where(((quarter + 1) & 2) == 0, value, -value)


def split(v):
    hi = v.astype(BF16)
    return hi, (v - hi.astype(F32)).astype(BF16)


def dot(a, b, dims=NN):
    return lax.dot_general(a, b, dims, preferred_element_type=F32)


def dot3(a, b, dims=NN):
    return dot(a[0], b[0], dims) + (dot(a[0], b[1], dims) + dot(a[1], b[0], dims))


def dot_exact(a, b, dims=NN):
    return lax.dot_general(a, b, dims, preferred_element_type=F32, precision=lax.Precision.HIGHEST)


def one_hot_product(rows, table):
    hi, lo = split(rows)
    n = rows.shape[0]
    both = dot(jnp.concatenate([hi, lo], axis=0), table)
    return both[:n] + both[n:]


def kernel(
    u_hbm, c_hbm, step_ref, w_hbm, pw_ref, bias_ref,
    out_hbm, dw_out, point_out, bias_out,
    u, cot, wv, pw, bv, pre, gp, ob,
    d1, d2, d3, d4, k1, k2, rep, rept, tile, tilet, bcol, onehot,
    ab, ul, xr, accp, accb,
    rs0, rcx, rs1, rz, mine, ag,
    dw, ry, dw1, rzl, dwf,
    small, scx, sz, sy, szl,
    local_sem, send_sem, recv_sem,
):
    dp = lax.axis_index("dp")
    sp = lax.axis_index("space")
    core = lax.rem(sp, 2)
    zh = lax.rem(sp // 2, 4)
    xx = sp // 8
    yy = dp // 4
    zl = lax.rem(dp, 4)

    def device(x=xx, z=zh, c=core, y=yy, l=zl):
        return (y * 4 + l, x * 8 + z * 2 + c)

    zl2 = lax.rem(zl + 2, 4)
    first = jnp.where(zl < 2, 1, 2)
    others = [(0, 1), (0, 2), (0, 3), (1, 0), (1, 1), (1, 2), (1, 3)]

    def plane(dc, d):
        return device(x=lax.rem(xx + d, 4), c=lax.rem(core + dc, 2))

    def owner_of(i):
        return device(z=lax.rem(zh + first + i, 4), l=zl2)

    def served(i):
        return device(z=lax.rem(zh + first + 5 - i, 4), l=zl2)

    def peer(axis, d):
        if axis == "y":
            return device(y=lax.rem(yy + d, 4))
        return device(l=lax.rem(zl + d, 4))

    loads = [
        pltpu.make_async_copy(u_hbm.at[0], u.at[0], local_sem.at[0]),
        pltpu.make_async_copy(u_hbm.at[1], u.at[1], local_sem.at[1]),
        pltpu.make_async_copy(c_hbm, cot, local_sem.at[2]),
        pltpu.make_async_copy(w_hbm, wv, local_sem.at[3]),
        pltpu.make_async_copy(pw_ref, pw, local_sem.at[7]),
        pltpu.make_async_copy(bias_ref, bv, local_sem.at[8]),
    ]
    for load in loads:
        load.start()

    barrier = pltpu.get_barrier_semaphore()
    greeted = [plane(*o) for o in others] + [owner_of(i) for i in range(4)]
    greeted += [peer(axis, d) for axis in ("y", "l") for d in (1, 2, 3)]
    for who in greeted:
        pl.semaphore_signal(barrier, inc=1, device_id=who, device_id_type=pl.DeviceIdType.MESH)

    row = iota((128, 256), 0)
    col = iota((128, 256), 1)
    base = wave((((row & 15) * (col & 63)) - 16 * (row >> 6)) * 64)
    hi, lo = split(jnp.where(((row >> 4) & 3) == (col >> 6), base, 0.0))
    d1[0:128], d1[128:256] = hi, lo

    row = iota((256, 256), 0)
    col = iota((256, 256), 1)
    owner = row >> 3
    owner_z = (zh + first + 2 * (owner >> 4) + (owner & 1)) & 3
    j = 2 * (((owner >> 1) & 3) * 8 + owner_z * 2 + ((owner >> 3) & 1)) + ((row >> 1) & 1)
    freq = jnp.where(j >= 32, j - 64, j)
    table = wave(freq * (sp * X + (col & 127)) + 1024 * ((row & 1) + (col >> 7)))
    turned = table.T
    for q in range(2):
        hi, lo = split(jnp.where(((row >> 2) & 1) == q, table, 0.0))
        d2[q, 0], d2[q, 1] = hi, lo
        hi, lo = split(jnp.where(((col >> 2) & 1) == q, turned, 0.0))
        d3[q, 0], d3[q, 1] = hi, lo

    count = [0]
    sends = []

    def start(src, dst, who):
        n = count[0]
        count[0] += 1
        copy = pltpu.make_async_remote_copy(
            src_ref=src, dst_ref=dst, send_sem=send_sem.at[n], recv_sem=recv_sem.at[n],
            device_id=who, device_id_type=pl.DeviceIdType.MESH,
        )
        copy.start()
        sends.append(copy)
        return n

    def arrived(n, dst):
        pltpu.make_async_remote_copy(
            src_ref=dst, dst_ref=dst, send_sem=send_sem.at[n], recv_sem=recv_sem.at[n],
            device_id=plane(1, 0), device_id_type=pl.DeviceIdType.MESH,
        ).wait_recv()

    def forward(s, wide, chain):
        def block(n, carry):
            if wide:
                v = jnp.concatenate(split(gp[s, pl.ds(4 * n, 4)].reshape(256, 128)), axis=1)
                both = dot(d1[...], v)
                out = both[:128, :128] + (both[128:, :128] + both[:128, 128:])
            else:
                both = dot(d1[...], u[s, pl.ds(4 * n, 4)].reshape(256, 128))
                out = both[:128] + both[128:]
            hi, lo = split(out)
            ab[s, 0, n, :, 0:128] = hi[:64]
            ab[s, 0, n, :, 128:256] = hi[64:]
            ab[s, 1, n, :, 0:128] = lo[:64]
            ab[s, 1, n, :, 128:256] = lo[64:]
            return carry

        lax.fori_loop(0, 8, block, 0)
        total = None
        for q in range(2):
            right = tuple(ab[s, p, 4 * q:4 * q + 4].reshape(256, 256) for p in range(2))
            part = dot3((d2[q, 0], d2[q, 1]), right, NT)
            total = part if total is None else total + part
        rs0[chain] = total.reshape(2, 2, 4, 2, 8, 256)

    def inverse(s, chain, finish):
        y = split(ag[chain].reshape(256, 256))
        for q in range(2):
            hi, lo = split(dot3((d3[q, 0], d3[q, 1]), y))
            for h in range(2):
                lanes = slice(128 * h, 128 * h + 128)
                for p, v in enumerate((hi, lo)):
                    ul[s, 2 * q + h, 128 * p:128 * p + 128, 0:128] = v[:128, lanes]
                    ul[s, 2 * q + h, 128 * p:128 * p + 128, 128:256] = v[128:, lanes]

        def block(n, carry):
            both = dot(d4[0], ul[s, n], NT)
            finish(n, both[:, :128] + (both[:, 128:] + dot(d4[1], ul[s, n, 0:128], NT)))
            return carry

        lax.fori_loop(0, 4, block, 0)

    mask16 = ((iota((16, 256), 1) & 15) == iota((16, 256), 0)).astype(F32)
    mask512 = ((iota((16, 512), 1) & 15) == iota((16, 512), 0)).astype(F32)

    def mix(s, own):
        spread = (own[:, None, :] * mask16[None]).reshape(128, 256)
        xr[s] = one_hot_product(spread, rep[...]).reshape(2, 2, 2, 16, 512)
        parts = []
        for b in range(2):
            re = jnp.zeros((16, 128), F32)
            im = jnp.zeros((16, 128), F32)
            for k in range(8):
                q, lanes = k // 4, slice(128 * (k % 4), 128 * (k % 4) + 128)
                whole = slice(128 * k, 128 * k + 128)
                x_re, x_im = xr[s, q, b, 0, :, lanes], xr[s, q, b, 1, :, lanes]
                w_re, w_im = wv[b, :, 0, whole], wv[b, :, 1, whole]
                re = re + (w_re * x_re - w_im * x_im)
                im = im + (w_re * x_im + w_im * x_re)
            parts += [re, im]
        wide = one_hot_product(jnp.concatenate(parts, axis=0), tilet[...])
        out = jnp.sum(wide.reshape(4, 16, 512) * mask512[None], axis=1)
        return jnp.concatenate([out[:, :256], out[:, 256:]], axis=0)

    def mix_back(s, own, after):
        spread = (own[:, None, :] * mask16[None]).reshape(128, 256)
        g = one_hot_product(spread[:64], tile[0]) + one_hot_product(spread[64:], tile[1])
        gs = [(g[32 * b:32 * b + 16], g[32 * b + 16:32 * b + 32]) for b in range(2)]
        for b in range(2):
            g_re, g_im = gs[b]
            for k in range(8):
                q, lanes = k // 4, slice(128 * (k % 4), 128 * (k % 4) + 128)
                x_re, x_im = xr[s, q, b, 0, :, lanes], xr[s, q, b, 1, :, lanes]
                at = (k // 2, slice(None), slice(128 * (k % 2), 128 * (k % 2) + 128))
                d_re = x_re * g_re + x_im * g_im
                d_im = x_re * g_im - x_im * g_re
                if s == 0:
                    dw[(2 * b,) + at] = d_re
                    dw[(2 * b + 1,) + at] = d_im
                else:
                    dw[(2 * b,) + at] += d_re
                    dw[(2 * b + 1,) + at] += d_im
        after()
        rows = [[None] * 8 for _ in range(2)]
        for b in range(2):
            g_re, g_im = gs[b]
            for k in range(8):
                whole = slice(128 * k, 128 * k + 128)
                w_re, w_im = wv[b, :, 0, whole], wv[b, :, 1, whole]
                rows[b][k] = (w_re * g_re + w_im * g_im, w_re * g_im - w_im * g_re)
        stacked = jnp.concatenate(
            [
                jnp.concatenate([rows[b][4 * q + k][p] for k in range(4)], axis=1)
                for q in range(2) for b in range(2) for p in range(2)
            ],
            axis=0,
        )
        wide = one_hot_product(stacked, rept[...])
        return jnp.sum(wide.reshape(8, 16, 256) * mask16[None], axis=1)

    def chain_of(s):
        for back in range(2):
            ch = 2 * s + back
            if back == 0:
                loads[s].wait()
                forward(s, False, ch)
                yield
            ns = [
                [start(rs0.at[ch, far, lax.rem(core + dc, 2), lax.rem(xx + d, 4)], rcx.at[ch, far, p], plane(dc, d))
                 for p, (dc, d) in enumerate(others)]
                for far in range(2)
            ]
            yield
            zs = []
            for far in range(2):
                total = rs0[ch, far, core, xx]
                for p in range(7):
                    arrived(ns[far][p], rcx.at[ch, far, p])
                    total = total + rcx[ch, far, p]
                rs1[ch, far] = total
                zs += [start(rs1.at[ch, far, k], rz.at[ch, 2 * far + k], owner_of(2 * far + k)) for k in range(2)]
                yield
            for i in (2, 3, 0, 1):
                arrived(zs[i], rz.at[ch, i])
            own = (rz[ch, 0] + rz[ch, 1]) + (rz[ch, 2] + rz[ch, 3])
            if back == 0:
                mine[ch] = mix(s, own * IN_SCALE) * OUT_SCALE
            else:
                mine[ch] = mix_back(s, own * OUT_SCALE, lambda: next(weights) if s == 1 else None) * IN_SCALE
            zs = [start(mine.at[ch], ag.at[ch, i // 2, core, xx, i % 2], served(i)) for i in range(4)]
            yield
            ns = [None, None]
            for far in (1, 0):
                for k in range(2):
                    arrived(zs[2 * far + k], ag.at[ch, far, core, xx, k])
                here = ag.at[ch, far, core, xx]
                ns[far] = [start(here, here, plane(dc, d)) for dc, d in others]
                yield
            for far in (1, 0):
                for p, (dc, d) in enumerate(others):
                    arrived(ns[far][p], ag.at[ch, far, lax.rem(core + dc, 2), lax.rem(xx + 4 - d, 4)])
            if back == 0:
                closure = step_ref[s]

                def finish(n, field):
                    rows = pl.ds(8 * n, 8)
                    p = field.reshape(8, 64, 128) + pre[s, rows]
                    sq = p * p
                    th = jnp.tanh(GELU_C * (p + 0.044715 * (sq * p)))
                    slope = 0.5 * (1.0 + th) + 0.5 * p * (1.0 - th * th) * (GELU_C * (1.0 + 3 * 0.044715 * sq))
                    live = (iota((8, 64, 128), 1) >= closure).astype(F32)
                    gp[s, rows] = cot[s, rows].astype(F32) * live * slope

                inverse(s, ch, finish)
                forward(s, True, ch + 1)
            else:

                def finish(n, field):
                    rows = pl.ds(8 * n, 8)
                    ob[s, rows] = (field.reshape(8, 64, 128) + pre[s, rows]).astype(BF16)

                inverse(s, ch, finish)
                pltpu.make_async_copy(ob.at[s], out_hbm.at[s], local_sem.at[4 + s]).start()

    def pointwise(s):
        def block(n, carry):
            v = u[s, :, pl.ds(16 * n, 16), :].astype(F32)
            for h in range(2):
                b = v[:, 8 * h:8 * h + 8].reshape(256, 128).astype(BF16)
                out = dot(k1[0], b) + dot(k1[1], b) + bcol[...]
                pre[s, :, pl.ds(16 * n + 8 * h, 8), :] = out.reshape(32, 8, 128)
            return carry

        lax.fori_loop(0, 4, block, 0)

    def point_back(s):
        def block(n, carry):
            v = u[s, :, pl.ds(16 * n, 16), :].astype(F32)
            for h in range(2):
                b = v[:, 8 * h:8 * h + 8].reshape(256, 128).astype(BF16)
                rows = pl.ds(16 * n + 8 * h, 8)
                g = gp[s, :, rows, :].reshape(256, 128)
                gs = split(g)
                pre[s, :, rows, :] = dot3((k2[0], k2[1]), gs).reshape(32, 8, 128)
                accp[...] += dot(b, gs[0], NT) + dot(b, gs[1], NT)
                accb[...] += g
            return carry

        lax.fori_loop(0, 4, block, 0)

    def later_tables():
        d4row = iota((64, 256), 0)
        d4col = iota((64, 256), 1)
        base = wave((((d4col & 15) * d4row) - 16 * (d4col >> 7)) * 64)
        for c in range(8):
            hi, lo = split(jnp.where(((d4col >> 4) & 7) == c, base, 0.0))
            d4[0, 64 * c:64 * c + 64] = hi
            d4[1, 64 * c:64 * c + 64] = lo
        rep[...] = ((iota((256, 512), 0) >> 4) == (iota((256, 512), 1) >> 5)).astype(BF16)
        rept[...] = ((iota((512, 256), 0) >> 5) == (iota((512, 256), 1) >> 4)).astype(BF16)
        for q in range(2):
            tile[q] = ((iota((256, 128), 0) >> 4) + 16 * q == (iota((256, 128), 1) & 31)).astype(BF16)
        tilet[...] = ((iota((128, 512), 0) & 31) == (iota((128, 512), 1) >> 4)).astype(BF16)

    def point_tables():
        pick = ((iota((256, 32), 0) >> 3) == iota((256, 32), 1)).astype(F32)
        onehot[...] = pick
        e = pick.astype(BF16)
        same = (iota((256, 256), 0) & 7) == (iota((256, 256), 1) & 7)
        for p, v in enumerate(split(pw[...])):
            k2[p] = jnp.where(same, dot(dot(e, v).astype(BF16), e, NT), 0.0).astype(BF16)
            k1[p] = jnp.where(same, dot(dot(e, v, NT).astype(BF16), e, NT), 0.0).astype(BF16)
        column = jnp.sum(pick * bv[...], axis=1, keepdims=True)
        bcol[...] = jnp.broadcast_to(column, (256, 128))
        accp[...] = jnp.zeros((256, 256), F32)
        accb[...] = jnp.zeros((256, 128), F32)

    def small_sum():
        same = ((iota((256, 256), 0) & 7) == (iota((256, 256), 1) & 7)).astype(F32)
        by_row = dot_exact(((iota((32, 256), 1) >> 3) == iota((32, 256), 0)).astype(F32), accp[...] * same)
        four = ((iota((256, 128), 0) >> 3) == (iota((256, 128), 1) & 31)).astype(F32)
        grid = dot_exact(by_row, four)
        grid = jnp.where((iota((32, 128), 0) & 3) == (iota((32, 128), 1) >> 5), grid, 0.0)
        small[0, 0:8] = dot_exact(((iota((8, 32), 1) >> 2) == iota((8, 32), 0)).astype(F32), grid)
        column = jnp.sum(accb[...], axis=1, keepdims=True)
        line = jnp.sum(column * four, axis=0, keepdims=True)
        small[0, 8:16] = jnp.broadcast_to(line, (8, 128))
        ns = [start(small.at[0], scx.at[p], plane(*o)) for p, o in enumerate(others)]
        yield
        total = small[0]
        for p in range(7):
            arrived(ns[p], scx.at[p])
            total = total + scx[p]
        small[1] = total
        ns = [start(small.at[1], sz.at[i], owner_of(i)) for i in range(4)]
        yield
        for i in range(4):
            arrived(ns[i], sz.at[i])
        small[2] = (sz[0] + sz[1]) + (sz[2] + sz[3])
        for k, (axis, got) in enumerate((("y", sy), ("l", szl))):
            ns = [start(small.at[2 + k], got.at[d - 1], peer(axis, d)) for d in (1, 2, 3)]
            yield
            for d in (1, 2, 3):
                arrived(ns[d - 1], got.at[d - 1])
            small[3 + k] = (small[2 + k] + got[0]) + (got[1] + got[2])
        total = small[4] * POINT_SCALE
        spread = dot_exact(((iota((32, 8), 0) >> 2) == iota((32, 8), 1)).astype(F32), total[0:8])
        spread = jnp.where((iota((32, 128), 0) & 3) == (iota((32, 128), 1) >> 5), spread, 0.0)
        point_out[...] = dot_exact(spread, ((iota((128, 32), 0) & 31) == iota((128, 32), 1)).astype(F32))
        bias_out[...] = total[8:9, 0:32]

    def weight_sum():
        near = [lax.rem(zl + d, 4) for d in range(4)]
        ns = {
            d: [start(dw.at[lax.rem(yy + e, 4), near[d]], ry.at[e - 1, d], peer("y", e)) for e in (1, 2, 3)]
            for d in (2, 1, 3, 0)
        }
        yield
        zs = {}
        for d in (2, 1, 3, 0):
            for e in (1, 2, 3):
                arrived(ns[d][e - 1], ry.at[e - 1, d])
            dw1[d] = (dw[yy, near[d]] + ry[0, d]) + (ry[1, d] + ry[2, d])
            if d > 0:
                zs[d] = start(dw1.at[d], rzl.at[d - 1], peer("l", d))
        yield
        for d in (1, 2, 3):
            arrived(zs[d], rzl.at[d - 1])
        dwf[yy, zl] = ((dw1[0] + rzl[0]) + (rzl[1] + rzl[2])) * SAMPLE_SCALE
        here = dwf.at[yy, zl]
        zs = {d: start(here, here, peer("l", d)) for d in (2, 1, 3)}
        ns = {0: [start(here, here, peer("y", e)) for e in (1, 2, 3)]}
        yield
        for d in (1, 3, 2):
            here = dwf.at[yy, lax.rem(zl + 4 - d, 4)]
            arrived(zs[d], here)
            ns[d] = [start(here, here, peer("y", e)) for e in (1, 2, 3)]
        yield
        for d in (0, 1, 3, 2):
            for e in (1, 2, 3):
                arrived(ns[d][e - 1], dwf.at[lax.rem(yy + 4 - e, 4), lax.rem(zl + 4 - d, 4)])
        pltpu.make_async_copy(dwf, dw_out, local_sem.at[6]).start()

    a, b = chain_of(0), chain_of(1)
    smalls, weights = small_sum(), weight_sum()

    def go(*parts):
        for part in parts:
            next(part, None)

    def sent(keep):
        done = len(sends) - keep
        for copy in sends[:done]:
            copy.wait_send()
        del sends[:done]

    go(a)
    pl.semaphore_wait(barrier, len(greeted))
    go(a)
    go(b)
    go(b)
    later_tables()
    go(a, a, b, b)
    loads[4].wait()
    loads[5].wait()
    point_tables()
    pointwise(0)
    pointwise(1)
    loads[3].wait()
    go(a, b)
    sent(16)
    go(a, b)
    go(a, b)
    loads[2].wait()
    go(a)
    go(b)
    go(a, a)
    point_back(0)
    go(b, b)
    point_back(1)
    go(smalls)
    sent(32)
    go(a, b)
    go(smalls)
    sent(28)
    go(weights)
    go(a, b)
    go(a, b)
    go(weights)
    go(smalls)
    go(a)
    go(weights)
    go(smalls)
    sent(18)
    go(b)
    go(smalls)
    go(weights)

    for copy in sends:
        copy.wait_send()
    pltpu.make_async_copy(ob.at[0], out_hbm.at[0], local_sem.at[4]).wait()
    pltpu.make_async_copy(ob.at[1], out_hbm.at[1], local_sem.at[5]).wait()
    pltpu.make_async_copy(dwf, dw_out, local_sem.at[6]).wait()


def place(grad, dw, point, bias, out, dw_out, point_out, bias_out, held, piece, whole, sem):
    loads = [pltpu.make_async_copy(grad.at[s], held.at[s], sem.at[s]) for s in range(2)]
    stores = [pltpu.make_async_copy(held.at[s], out.at[s], sem.at[2 + s]) for s in range(2)]
    load = pltpu.make_async_copy(dw, piece, sem.at[4])
    store = pltpu.make_async_copy(whole, dw_out, sem.at[5])
    load.start()
    for copy in loads:
        copy.start()
    point_out[...] = point[...]
    bias_out[...] = bias[...]
    load.wait()
    for b in range(2):
        for p in range(2):
            for q in range(4):
                whole[b, :, p, 256 * q:256 * q + 256] = piece[2 * b + p, q]
    store.start()
    for s in range(2):
        loads[s].wait()
        stores[s].start()
    for copy in [store] + stores:
        copy.wait()


COPIES = 4 * 36 + 17 + 30


def body(layer_input, cotangent, closure_step, spectral_weight, point_weight, bias):
    anywhere = pl.BlockSpec(memory_space=pl.ANY)
    vmem = pl.BlockSpec(memory_space=pltpu.VMEM)
    V = pltpu.VMEM
    scratch = [
        V((S, C, T, X), BF16), V((S, C, T, X), BF16), V((2, 16, 2, 1024), F32), V((C, C), F32), V((1, C), F32),
        V((S, C, T, X), F32), V((S, C, T, X), F32), V((S, C, T, X), BF16),
        V((256, 256), BF16), V((2, 2, 256, 256), BF16), V((2, 2, 256, 256), BF16), V((2, 512, 256), BF16),
        V((2, 256, 256), BF16), V((2, 256, 256), BF16),
        V((256, 512), BF16), V((512, 256), BF16), V((2, 256, 128), BF16), V((128, 512), BF16),
        V((256, 128), F32), V((256, 32), F32),
        V((S, 2, 8, 64, 256), BF16), V((S, 4, 256, 256), BF16), V((S, 2, 2, 2, 16, 512), F32),
        V((256, 256), F32), V((256, 128), F32),
        V((4, 2, 2, 4, 2, 8, 256), F32), V((4, 2, 7, 2, 8, 256), F32), V((4, 2, 2, 8, 256), F32),
        V((4, 4, 8, 256), F32), V((4, 8, 256), F32), V((4, 2, 2, 4, 2, 8, 256), F32),
        V((4, 4, 16, 256), F32), V((3, 4, 16, 256), F32), V((4, 16, 256), F32), V((3, 16, 256), F32),
        V((4, 4, 16, 256), F32),
        V((5, 16, 128), F32), V((7, 16, 128), F32), V((4, 16, 128), F32), V((3, 16, 128), F32), V((3, 16, 128), F32),
        pltpu.SemaphoreType.DMA((9,)), pltpu.SemaphoreType.DMA((COPIES,)), pltpu.SemaphoreType.DMA((COPIES,)),
    ]
    grad, dw, point, bias_grad = pl.pallas_call(
        kernel,
        out_shape=(
            jax.ShapeDtypeStruct((S, C, T, X), BF16),
            jax.ShapeDtypeStruct((4, 4, 16, 256), F32),
            jax.ShapeDtypeStruct((C, C), F32),
            jax.ShapeDtypeStruct((1, C), F32),
        ),
        in_specs=[anywhere, anywhere, pl.BlockSpec(memory_space=pltpu.SMEM), anywhere, anywhere, anywhere],
        out_specs=(anywhere, anywhere, vmem, vmem),
        scratch_shapes=scratch,
        compiler_params=pltpu.CompilerParams(
            collective_id=0, has_side_effects=True, vmem_limit_bytes=60 * 1024 * 1024
        ),
    )(layer_input, cotangent, closure_step, spectral_weight, point_weight, bias.reshape(1, C))
    grad, dw, point, bias_grad = pl.pallas_call(
        place,
        out_shape=(
            jax.ShapeDtypeStruct((S, C, T, X), BF16),
            jax.ShapeDtypeStruct((2, 16, 2, 1024), F32),
            jax.ShapeDtypeStruct((C, C), F32),
            jax.ShapeDtypeStruct((1, C), F32),
        ),
        in_specs=[anywhere, anywhere, vmem, vmem],
        out_specs=(anywhere, anywhere, vmem, vmem),
        scratch_shapes=[
            V((S, C, T, X), BF16), V((4, 4, 16, 256), F32), V((2, 16, 2, 1024), F32), pltpu.SemaphoreType.DMA((6,)),
        ],
        compiler_params=pltpu.CompilerParams(vmem_limit_bytes=60 * 1024 * 1024),
    )(grad, dw, point, bias_grad)
    return grad, dw, point, bias_grad.reshape(C)


def solution(mesh):
    return jax.shard_map(
        body,
        mesh=mesh,
        in_specs=(
            P("dp", None, None, "space"),
            P("dp", None, None, "space"),
            P("dp"),
            P("space", None, None, None),
            P(),
            P(),
        ),
        out_specs=(P("dp", None, None, "space"), P("space", None, None, None), P(), P()),
        check_vma=False,
    )
```

```python
import functools
import math

import jax
import jax.numpy as jnp
from jax import lax
from jax.experimental import pallas as pl
from jax.experimental.pallas import tpu as pltpu
from jax.sharding import PartitionSpec as P

F32 = jnp.float32
BF16 = jnp.bfloat16
S, C, T, X, M = 2, 32, 64, 128, 16
GROUPS = 32
NX = X * GROUPS
NN = (((1,), (0,)), ((), ()))
NT = (((1,), (1,)), ((), ()))
TWO_PI = 2.0 * math.pi
POINT_SCALE = 1.0 / math.sqrt(32 * T * NX)
SAMPLE_SCALE = 1.0 / math.sqrt(32)
IN_SCALE = 1.0 / 512.0
OUT_SCALE = 1.0 / 32.0
GELU_C = math.sqrt(2.0 / math.pi)


def iota(shape, axis):
    return lax.broadcasted_iota(jnp.int32, shape, axis)


def wave(turn):
    near = turn + 512
    t = ((near & 1023) - 512).astype(F32) * (TWO_PI / NX)
    quarter = (near >> 10) & 3
    sq = t * t
    even = 1.0 + sq * (-1 / 2 + sq * (1 / 24 + sq * (-1 / 720 + sq * (1 / 40320))))
    odd = t * (1.0 + sq * (-1 / 6 + sq * (1 / 120 + sq * (-1 / 5040 + sq * (1 / 362880)))))
    value = jnp.where((quarter & 1) == 0, even, odd)
    return jnp.where(((quarter + 1) & 2) == 0, value, -value)


def split(v):
    hi = v.astype(BF16)
    return hi, (v - hi.astype(F32)).astype(BF16)


def dot(a, b, dims=NN):
    return lax.dot_general(a, b, dims, preferred_element_type=F32)


def dot3(a, b, dims=NN):
    return dot(a[0], b[0], dims) + (dot(a[0], b[1], dims) + dot(a[1], b[0], dims))


def dot_exact(a, b, dims=NN):
    return lax.dot_general(a, b, dims, preferred_element_type=F32, precision=lax.Precision.HIGHEST)


def one_hot_product(rows, table):
    hi, lo = split(rows)
    n = rows.shape[0]
    both = dot(jnp.concatenate([hi, lo], axis=0), table)
    return both[:n] + both[n:]


def kernel(
    u_hbm, c_hbm, step_ref, w_hbm, pw_ref, bias_ref,
    out_hbm, dw_out, point_out, bias_out,
    u, cot, wv, pw, bv, pre, gp, ob,
    d1, d2, d3, d4, k1, k2, rep, rept, tile, tilet, bcol, onehot,
    ab, ul, xr, accp, accb,
    rs0, rcx, rs1, rz, mine, ag,
    dw, ry, dw1, rzl, dwf,
    small, scx, sz, sy, szl,
    local_sem, send_sem, recv_sem,
):
    dp = lax.axis_index("dp")
    sp = lax.axis_index("space")
    core = lax.rem(sp, 2)
    zh = lax.rem(sp // 2, 4)
    xx = sp // 8
    yy = dp // 4
    zl = lax.rem(dp, 4)

    def device(x=xx, z=zh, c=core, y=yy, l=zl):
        return (y * 4 + l, x * 8 + z * 2 + c)

    zl2 = lax.rem(zl + 2, 4)
    first = jnp.where(zl < 2, 1, 2)
    others = [(0, 1), (0, 2), (0, 3), (1, 0), (1, 1), (1, 2), (1, 3)]

    def plane(dc, d):
        return device(x=lax.rem(xx + d, 4), c=lax.rem(core + dc, 2))

    def owner_of(i):
        return device(z=lax.rem(zh + first + i, 4), l=zl2)

    def served(i):
        return device(z=lax.rem(zh + first + 5 - i, 4), l=zl2)

    def peer(axis, d):
        if axis == "y":
            return device(y=lax.rem(yy + d, 4))
        return device(l=lax.rem(zl + d, 4))

    loads = [
        pltpu.make_async_copy(u_hbm.at[0], u.at[0], local_sem.at[0]),
        pltpu.make_async_copy(u_hbm.at[1], u.at[1], local_sem.at[1]),
        pltpu.make_async_copy(c_hbm, cot, local_sem.at[2]),
        pltpu.make_async_copy(w_hbm, wv, local_sem.at[3]),
        pltpu.make_async_copy(pw_ref, pw, local_sem.at[7]),
        pltpu.make_async_copy(bias_ref, bv, local_sem.at[8]),
    ]
    for load in loads:
        load.start()

    barrier = pltpu.get_barrier_semaphore()
    greeted = [plane(*o) for o in others] + [owner_of(i) for i in range(4)]
    greeted += [peer(axis, d) for axis in ("y", "l") for d in (1, 2, 3)]
    for who in greeted:
        pl.semaphore_signal(barrier, inc=1, device_id=who, device_id_type=pl.DeviceIdType.MESH)

    row = iota((128, 256), 0)
    col = iota((128, 256), 1)
    base = wave((((row & 15) * (col & 63)) - 16 * (row >> 6)) * 64)
    hi, lo = split(jnp.where(((row >> 4) & 3) == (col >> 6), base, 0.0))
    d1[0:128], d1[128:256] = hi, lo

    row = iota((256, 256), 0)
    col = iota((256, 256), 1)
    owner = row >> 3
    owner_z = (zh + first + 2 * (owner >> 4) + (owner & 1)) & 3
    j = 2 * (((owner >> 1) & 3) * 8 + owner_z * 2 + ((owner >> 3) & 1)) + ((row >> 1) & 1)
    freq = jnp.where(j >= 32, j - 64, j)
    table = wave(freq * (sp * X + (col & 127)) + 1024 * ((row & 1) + (col >> 7)))
    turned = table.T
    for q in range(2):
        hi, lo = split(jnp.where(((row >> 2) & 1) == q, table, 0.0))
        d2[q, 0], d2[q, 1] = hi, lo
        hi, lo = split(jnp.where(((col >> 2) & 1) == q, turned, 0.0))
        d3[q, 0], d3[q, 1] = hi, lo

    count = [0]
    sends = []

    def start(src, dst, who):
        n = count[0]
        count[0] += 1
        copy = pltpu.make_async_remote_copy(
            src_ref=src, dst_ref=dst, send_sem=send_sem.at[n], recv_sem=recv_sem.at[n],
            device_id=who, device_id_type=pl.DeviceIdType.MESH,
        )
        copy.start()
        sends.append(copy)
        return n

    def arrived(n, dst):
        pltpu.make_async_remote_copy(
            src_ref=dst, dst_ref=dst, send_sem=send_sem.at[n], recv_sem=recv_sem.at[n],
            device_id=plane(1, 0), device_id_type=pl.DeviceIdType.MESH,
        ).wait_recv()

    def forward(s, wide, chain):
        def block(n, carry):
            if wide:
                v = jnp.concatenate(split(gp[s, pl.ds(4 * n, 4)].reshape(256, 128)), axis=1)
                both = dot(d1[...], v)
                out = both[:128, :128] + (both[128:, :128] + both[:128, 128:])
            else:
                both = dot(d1[...], u[s, pl.ds(4 * n, 4)].reshape(256, 128))
                out = both[:128] + both[128:]
            hi, lo = split(out)
            ab[s, 0, n, :, 0:128] = hi[:64]
            ab[s, 0, n, :, 128:256] = hi[64:]
            ab[s, 1, n, :, 0:128] = lo[:64]
            ab[s, 1, n, :, 128:256] = lo[64:]
            return carry

        lax.fori_loop(0, 4, lambda n, carry: block(2 * n + 1, block(2 * n, carry)), 0)
        total = None
        for q in range(2):
            right = tuple(ab[s, p, 4 * q:4 * q + 4].reshape(256, 256) for p in range(2))
            part = dot3((d2[q, 0], d2[q, 1]), right, NT)
            total = part if total is None else total + part
        rs0[chain] = total.reshape(2, 2, 4, 2, 8, 256)

    def inverse(s, chain, finish):
        y = split(ag[chain].reshape(256, 256))
        for q in range(2):
            hi, lo = split(dot3((d3[q, 0], d3[q, 1]), y))
            for h in range(2):
                lanes = slice(128 * h, 128 * h + 128)
                for p, v in enumerate((hi, lo)):
                    ul[s, 2 * q + h, 128 * p:128 * p + 128, 0:128] = v[:128, lanes]
                    ul[s, 2 * q + h, 128 * p:128 * p + 128, 128:256] = v[128:, lanes]

        def block(n, carry):
            both = dot(d4[0], ul[s, n], NT)
            finish(n, both[:, :128] + (both[:, 128:] + dot(d4[1], ul[s, n, 0:128], NT)))
            return carry

        lax.fori_loop(0, 2, lambda n, carry: block(2 * n + 1, block(2 * n, carry)), 0)

    mask16 = ((iota((16, 256), 1) & 15) == iota((16, 256), 0)).astype(F32)
    mask512 = ((iota((16, 512), 1) & 15) == iota((16, 512), 0)).astype(F32)

    def mix(s, own):
        spread = (own[:, None, :] * mask16[None]).reshape(128, 256)
        xr[s] = one_hot_product(spread, rep[...]).reshape(2, 2, 2, 16, 512)
        parts = []
        for b in range(2):
            re = jnp.zeros((16, 128), F32)
            im = jnp.zeros((16, 128), F32)
            for k in range(8):
                q, lanes = k // 4, slice(128 * (k % 4), 128 * (k % 4) + 128)
                whole = slice(128 * k, 128 * k + 128)
                x_re, x_im = xr[s, q, b, 0, :, lanes], xr[s, q, b, 1, :, lanes]
                w_re, w_im = wv[b, :, 0, whole], wv[b, :, 1, whole]
                re = re + (w_re * x_re - w_im * x_im)
                im = im + (w_re * x_im + w_im * x_re)
            parts += [re, im]
        wide = one_hot_product(jnp.concatenate(parts, axis=0), tilet[...])
        out = jnp.sum(wide.reshape(4, 16, 512) * mask512[None], axis=1)
        return jnp.concatenate([out[:, :256], out[:, 256:]], axis=0)

    def mix_back(s, own, after):
        spread = (own[:, None, :] * mask16[None]).reshape(128, 256)
        g = one_hot_product(spread[:64], tile[0]) + one_hot_product(spread[64:], tile[1])
        gs = [(g[32 * b:32 * b + 16], g[32 * b + 16:32 * b + 32]) for b in range(2)]
        for b in range(2):
            g_re, g_im = gs[b]
            for k in range(8):
                q, lanes = k // 4, slice(128 * (k % 4), 128 * (k % 4) + 128)
                x_re, x_im = xr[s, q, b, 0, :, lanes], xr[s, q, b, 1, :, lanes]
                at = (k // 2, slice(None), slice(128 * (k % 2), 128 * (k % 2) + 128))
                d_re = x_re * g_re + x_im * g_im
                d_im = x_re * g_im - x_im * g_re
                if s == 0:
                    dw[(2 * b,) + at] = d_re
                    dw[(2 * b + 1,) + at] = d_im
                else:
                    dw[(2 * b,) + at] += d_re
                    dw[(2 * b + 1,) + at] += d_im
        after()
        rows = [[None] * 8 for _ in range(2)]
        for b in range(2):
            g_re, g_im = gs[b]
            for k in range(8):
                whole = slice(128 * k, 128 * k + 128)
                w_re, w_im = wv[b, :, 0, whole], wv[b, :, 1, whole]
                rows[b][k] = (w_re * g_re + w_im * g_im, w_re * g_im - w_im * g_re)
        stacked = jnp.concatenate(
            [
                jnp.concatenate([rows[b][4 * q + k][p] for k in range(4)], axis=1)
                for q in range(2) for b in range(2) for p in range(2)
            ],
            axis=0,
        )
        wide = one_hot_product(stacked, rept[...])
        return jnp.sum(wide.reshape(8, 16, 256) * mask16[None], axis=1)

    def chain_of(s):
        for back in range(2):
            ch = 2 * s + back
            if back == 0:
                loads[s].wait()
                forward(s, False, ch)
                yield
            ns = [
                [start(rs0.at[ch, far, lax.rem(core + dc, 2), lax.rem(xx + d, 4)], rcx.at[ch, far, p], plane(dc, d))
                 for p, (dc, d) in enumerate(others)]
                for far in range(2)
            ]
            yield
            zs = []
            for far in range(2):
                total = rs0[ch, far, core, xx]
                for p in range(7):
                    arrived(ns[far][p], rcx.at[ch, far, p])
                    total = total + rcx[ch, far, p]
                rs1[ch, far] = total
                zs += [start(rs1.at[ch, far, k], rz.at[ch, 2 * far + k], owner_of(2 * far + k)) for k in range(2)]
                yield
            for i in (2, 3, 0, 1):
                arrived(zs[i], rz.at[ch, i])
            own = (rz[ch, 0] + rz[ch, 1]) + (rz[ch, 2] + rz[ch, 3])
            if back == 0:
                mine[ch] = mix(s, own * IN_SCALE) * OUT_SCALE
            else:
                mine[ch] = mix_back(s, own * OUT_SCALE, lambda: next(weights) if s == 1 else None) * IN_SCALE
            zs = [start(mine.at[ch], ag.at[ch, i // 2, core, xx, i % 2], served(i)) for i in range(4)]
            yield
            ns = [None, None]
            for far in (1, 0):
                for k in range(2):
                    arrived(zs[2 * far + k], ag.at[ch, far, core, xx, k])
                here = ag.at[ch, far, core, xx]
                ns[far] = [start(here, here, plane(dc, d)) for dc, d in others]
                yield
            for far in (1, 0):
                for p, (dc, d) in enumerate(others):
                    arrived(ns[far][p], ag.at[ch, far, lax.rem(core + dc, 2), lax.rem(xx + 4 - d, 4)])
            if back == 0:
                closure = step_ref[s]

                def finish(n, field):
                    rows = pl.ds(8 * n, 8)
                    p = field.reshape(8, 64, 128) + pre[s, rows]
                    sq = p * p
                    th = jnp.tanh(GELU_C * (p + 0.044715 * (sq * p)))
                    slope = 0.5 * (1.0 + th) + 0.5 * p * (1.0 - th * th) * (GELU_C * (1.0 + 3 * 0.044715 * sq))
                    live = (iota((8, 64, 128), 1) >= closure).astype(F32)
                    gp[s, rows] = cot[s, rows].astype(F32) * live * slope

                inverse(s, ch, finish)
                forward(s, True, ch + 1)
            else:

                def finish(n, field):
                    rows = pl.ds(8 * n, 8)
                    ob[s, rows] = (field.reshape(8, 64, 128) + pre[s, rows]).astype(BF16)

                inverse(s, ch, finish)
                pltpu.make_async_copy(ob.at[s], out_hbm.at[s], local_sem.at[4 + s]).start()

    def pointwise(s):
        def block(n, carry):
            v = u[s, :, pl.ds(16 * n, 16), :].astype(F32)
            for h in range(2):
                b = v[:, 8 * h:8 * h + 8].reshape(256, 128).astype(BF16)
                out = dot(k1[0], b) + dot(k1[1], b) + bcol[...]
                pre[s, :, pl.ds(16 * n + 8 * h, 8), :] = out.reshape(32, 8, 128)
            return carry

        lax.fori_loop(0, 4, block, 0)

    def point_back(s):
        def block(n, carry):
            v = u[s, :, pl.ds(16 * n, 16), :].astype(F32)
            for h in range(2):
                b = v[:, 8 * h:8 * h + 8].reshape(256, 128).astype(BF16)
                rows = pl.ds(16 * n + 8 * h, 8)
                g = gp[s, :, rows, :].reshape(256, 128)
                gs = split(g)
                pre[s, :, rows, :] = dot3((k2[0], k2[1]), gs).reshape(32, 8, 128)
                accp[...] += dot(b, gs[0], NT) + dot(b, gs[1], NT)
                accb[...] += g
            return carry

        lax.fori_loop(0, 4, block, 0)

    def later_tables():
        d4row = iota((64, 256), 0)
        d4col = iota((64, 256), 1)
        base = wave((((d4col & 15) * d4row) - 16 * (d4col >> 7)) * 64)
        for c in range(8):
            hi, lo = split(jnp.where(((d4col >> 4) & 7) == c, base, 0.0))
            d4[0, 64 * c:64 * c + 64] = hi
            d4[1, 64 * c:64 * c + 64] = lo
        rep[...] = ((iota((256, 512), 0) >> 4) == (iota((256, 512), 1) >> 5)).astype(BF16)
        rept[...] = ((iota((512, 256), 0) >> 5) == (iota((512, 256), 1) >> 4)).astype(BF16)
        for q in range(2):
            tile[q] = ((iota((256, 128), 0) >> 4) + 16 * q == (iota((256, 128), 1) & 31)).astype(BF16)
        tilet[...] = ((iota((128, 512), 0) & 31) == (iota((128, 512), 1) >> 4)).astype(BF16)

    def point_tables():
        pick = ((iota((256, 32), 0) >> 3) == iota((256, 32), 1)).astype(F32)
        onehot[...] = pick
        e = pick.astype(BF16)
        same = (iota((256, 256), 0) & 7) == (iota((256, 256), 1) & 7)
        for p, v in enumerate(split(pw[...])):
            k2[p] = jnp.where(same, dot(dot(e, v).astype(BF16), e, NT), 0.0).astype(BF16)
            k1[p] = jnp.where(same, dot(dot(e, v, NT).astype(BF16), e, NT), 0.0).astype(BF16)
        column = jnp.sum(pick * bv[...], axis=1, keepdims=True)
        bcol[...] = jnp.broadcast_to(column, (256, 128))
        accp[...] = jnp.zeros((256, 256), F32)
        accb[...] = jnp.zeros((256, 128), F32)

    def small_sum():
        same = ((iota((256, 256), 0) & 7) == (iota((256, 256), 1) & 7)).astype(F32)
        by_row = dot_exact(((iota((32, 256), 1) >> 3) == iota((32, 256), 0)).astype(F32), accp[...] * same)
        four = ((iota((256, 128), 0) >> 3) == (iota((256, 128), 1) & 31)).astype(F32)
        grid = dot_exact(by_row, four)
        grid = jnp.where((iota((32, 128), 0) & 3) == (iota((32, 128), 1) >> 5), grid, 0.0)
        small[0, 0:8] = dot_exact(((iota((8, 32), 1) >> 2) == iota((8, 32), 0)).astype(F32), grid)
        column = jnp.sum(accb[...], axis=1, keepdims=True)
        line = jnp.sum(column * four, axis=0, keepdims=True)
        small[0, 8:16] = jnp.broadcast_to(line, (8, 128))
        ns = [start(small.at[0], scx.at[p], plane(*o)) for p, o in enumerate(others)]
        yield
        total = small[0]
        for p in range(7):
            arrived(ns[p], scx.at[p])
            total = total + scx[p]
        small[1] = total
        ns = [start(small.at[1], sz.at[i], owner_of(i)) for i in range(4)]
        yield
        for i in range(4):
            arrived(ns[i], sz.at[i])
        small[2] = (sz[0] + sz[1]) + (sz[2] + sz[3])
        for k, (axis, got) in enumerate((("y", sy), ("l", szl))):
            ns = [start(small.at[2 + k], got.at[d - 1], peer(axis, d)) for d in (1, 2, 3)]
            yield
            for d in (1, 2, 3):
                arrived(ns[d - 1], got.at[d - 1])
            small[3 + k] = (small[2 + k] + got[0]) + (got[1] + got[2])
        total = small[4] * POINT_SCALE
        spread = dot_exact(((iota((32, 8), 0) >> 2) == iota((32, 8), 1)).astype(F32), total[0:8])
        spread = jnp.where((iota((32, 128), 0) & 3) == (iota((32, 128), 1) >> 5), spread, 0.0)
        point_out[...] = dot_exact(spread, ((iota((128, 32), 0) & 31) == iota((128, 32), 1)).astype(F32))
        bias_out[...] = total[8:9, 0:32]

    def weight_sum():
        near = [lax.rem(zl + d, 4) for d in range(4)]
        ns = {
            d: [start(dw.at[lax.rem(yy + e, 4), near[d]], ry.at[e - 1, d], peer("y", e)) for e in (1, 2, 3)]
            for d in (2, 1, 3, 0)
        }
        yield
        zs = {}
        for d in (2, 1, 3, 0):
            for e in (1, 2, 3):
                arrived(ns[d][e - 1], ry.at[e - 1, d])
            dw1[d] = (dw[yy, near[d]] + ry[0, d]) + (ry[1, d] + ry[2, d])
            if d > 0:
                zs[d] = start(dw1.at[d], rzl.at[d - 1], peer("l", d))
        yield
        for d in (1, 2, 3):
            arrived(zs[d], rzl.at[d - 1])
        dwf[yy, zl] = ((dw1[0] + rzl[0]) + (rzl[1] + rzl[2])) * SAMPLE_SCALE
        here = dwf.at[yy, zl]
        zs = {d: start(here, here, peer("l", d)) for d in (2, 1, 3)}
        ns = {0: [start(here, here, peer("y", e)) for e in (1, 2, 3)]}
        yield
        for d in (1, 3, 2):
            here = dwf.at[yy, lax.rem(zl + 4 - d, 4)]
            arrived(zs[d], here)
            ns[d] = [start(here, here, peer("y", e)) for e in (1, 2, 3)]
        yield
        for d in (0, 1, 3, 2):
            for e in (1, 2, 3):
                arrived(ns[d][e - 1], dwf.at[lax.rem(yy + 4 - e, 4), lax.rem(zl + 4 - d, 4)])
        pltpu.make_async_copy(dwf, dw_out, local_sem.at[6]).start()

    a, b = chain_of(0), chain_of(1)
    smalls, weights = small_sum(), weight_sum()

    def go(*parts):
        for part in parts:
            next(part, None)

    def sent(keep):
        done = len(sends) - keep
        for copy in sends[:done]:
            copy.wait_send()
        del sends[:done]

    go(a)
    pl.semaphore_wait(barrier, len(greeted))
    go(a)
    go(b)
    go(b)
    later_tables()
    go(a, a, b, b)
    loads[4].wait()
    loads[5].wait()
    point_tables()
    pointwise(0)
    pointwise(1)
    loads[3].wait()
    go(a, b)
    sent(16)
    go(a, b)
    go(a, b)
    loads[2].wait()
    go(a)
    go(b)
    go(a, a)
    point_back(0)
    go(b, b)
    point_back(1)
    go(smalls)
    sent(32)
    go(a, b)
    go(smalls)
    sent(28)
    go(weights)
    go(a, b)
    go(a, b)
    go(weights)
    go(smalls)
    go(a)
    go(weights)
    go(smalls)
    sent(18)
    go(b)
    go(weights)
    go(smalls)

    for copy in sends:
        copy.wait_send()
    pltpu.make_async_copy(ob.at[0], out_hbm.at[0], local_sem.at[4]).wait()
    pltpu.make_async_copy(ob.at[1], out_hbm.at[1], local_sem.at[5]).wait()
    pltpu.make_async_copy(dwf, dw_out, local_sem.at[6]).wait()


def place(grad, dw, point, bias, out, dw_out, point_out, bias_out, held, piece, whole, sem):
    loads = [pltpu.make_async_copy(grad.at[s], held.at[s], sem.at[s]) for s in range(2)]
    stores = [pltpu.make_async_copy(held.at[s], out.at[s], sem.at[2 + s]) for s in range(2)]
    load = pltpu.make_async_copy(dw, piece, sem.at[4])
    store = pltpu.make_async_copy(whole, dw_out, sem.at[5])
    load.start()
    for copy in loads:
        copy.start()
    point_out[...] = point[...]
    bias_out[...] = bias[...]
    load.wait()
    for b in range(2):
        for p in range(2):
            for q in range(4):
                whole[b, :, p, 256 * q:256 * q + 256] = piece[2 * b + p, q]
    store.start()
    for s in range(2):
        loads[s].wait()
        stores[s].start()
    for copy in [store] + stores:
        copy.wait()


COPIES = 4 * 36 + 17 + 30


def body(layer_input, cotangent, closure_step, spectral_weight, point_weight, bias):
    anywhere = pl.BlockSpec(memory_space=pl.ANY)
    vmem = pl.BlockSpec(memory_space=pltpu.VMEM)
    V = pltpu.VMEM
    scratch = [
        V((S, C, T, X), BF16), V((S, C, T, X), BF16), V((2, 16, 2, 1024), F32), V((C, C), F32), V((1, C), F32),
        V((S, C, T, X), F32), V((S, C, T, X), F32), V((S, C, T, X), BF16),
        V((256, 256), BF16), V((2, 2, 256, 256), BF16), V((2, 2, 256, 256), BF16), V((2, 512, 256), BF16),
        V((2, 256, 256), BF16), V((2, 256, 256), BF16),
        V((256, 512), BF16), V((512, 256), BF16), V((2, 256, 128), BF16), V((128, 512), BF16),
        V((256, 128), F32), V((256, 32), F32),
        V((S, 2, 8, 64, 256), BF16), V((S, 4, 256, 256), BF16), V((S, 2, 2, 2, 16, 512), F32),
        V((256, 256), F32), V((256, 128), F32),
        V((4, 2, 2, 4, 2, 8, 256), F32), V((4, 2, 7, 2, 8, 256), F32), V((4, 2, 2, 8, 256), F32),
        V((4, 4, 8, 256), F32), V((4, 8, 256), F32), V((4, 2, 2, 4, 2, 8, 256), F32),
        V((4, 4, 16, 256), F32), V((3, 4, 16, 256), F32), V((4, 16, 256), F32), V((3, 16, 256), F32),
        V((4, 4, 16, 256), F32),
        V((5, 16, 128), F32), V((7, 16, 128), F32), V((4, 16, 128), F32), V((3, 16, 128), F32), V((3, 16, 128), F32),
        pltpu.SemaphoreType.DMA((9,)), pltpu.SemaphoreType.DMA((COPIES,)), pltpu.SemaphoreType.DMA((COPIES,)),
    ]
    grad, dw, point, bias_grad = pl.pallas_call(
        kernel,
        out_shape=(
            jax.ShapeDtypeStruct((S, C, T, X), BF16),
            jax.ShapeDtypeStruct((4, 4, 16, 256), F32),
            jax.ShapeDtypeStruct((C, C), F32),
            jax.ShapeDtypeStruct((1, C), F32),
        ),
        in_specs=[anywhere, anywhere, pl.BlockSpec(memory_space=pltpu.SMEM), anywhere, anywhere, anywhere],
        out_specs=(anywhere, anywhere, vmem, vmem),
        scratch_shapes=scratch,
        compiler_params=pltpu.CompilerParams(
            collective_id=0, has_side_effects=True, vmem_limit_bytes=60 * 1024 * 1024
        ),
    )(layer_input, cotangent, closure_step, spectral_weight, point_weight, bias.reshape(1, C))
    grad, dw, point, bias_grad = pl.pallas_call(
        place,
        out_shape=(
            jax.ShapeDtypeStruct((S, C, T, X), BF16),
            jax.ShapeDtypeStruct((2, 16, 2, 1024), F32),
            jax.ShapeDtypeStruct((C, C), F32),
            jax.ShapeDtypeStruct((1, C), F32),
        ),
        in_specs=[anywhere, anywhere, vmem, vmem],
        out_specs=(anywhere, anywhere, vmem, vmem),
        scratch_shapes=[
            V((S, C, T, X), BF16), V((4, 4, 16, 256), F32), V((2, 16, 2, 1024), F32), pltpu.SemaphoreType.DMA((6,)),
        ],
        compiler_params=pltpu.CompilerParams(vmem_limit_bytes=60 * 1024 * 1024),
    )(grad, dw, point, bias_grad)
    return grad, dw, point, bias_grad.reshape(C)


def solution(mesh):
    return jax.shard_map(
        body,
        mesh=mesh,
        in_specs=(
            P("dp", None, None, "space"),
            P("dp", None, None, "space"),
            P("dp"),
            P("space", None, None, None),
            P(),
            P(),
        ),
        out_specs=(P("dp", None, None, "space"), P("space", None, None, None), P(), P()),
        check_vma=False,
    )
```
